32 devices in a mesh: parts: 2 (over x), blk: 8 (over z, y), heads: 2 (over core).
Axes of the slice: x: 2, y: 2, z: 4, core: 2. Of those that a mesh axis runs over, the one named last changes fastest.
Arguments:
- frames: bfloat16 [12288, 1024], P(('parts', 'blk', 'heads')), parts along dimension 0, may hold values from -6 to 6
- modulation: float32 [6, 1024], P('parts'), parts along dimension 0, may hold values from -3 to 3
- w_qkv: bfloat16 [1024, 3072], replicated, may hold values from -4 to 4
- w_out: bfloat16 [1024, 1024], replicated, may hold values from -0.1875 to 0.1875
- turn_id: int32 [96], P('parts'), parts along dimension 0, may hold values from 0 to 11, never falling along the last dimension, each value on 1 to 12 neighbouring positions
- speaker: int32 [96], P('parts'), parts along dimension 0, may hold values from 0 to 3
- ref_flag: int32 [96], P('parts'), parts along dimension 0, may hold values from 0 to 1, as said below
Outputs:
- mixed: bfloat16 [12288, 1024], P(('parts', 'blk', 'heads')), parts along dimension 0
The draws below stay inside these ranges and needn't reach their ends.
There are 2 independent parts, one for each index of `parts`. The reference program is written for one: setup_inputs(seed, part) draws one part's arguments, and reference() takes and returns one part's arrays. A program takes and returns all parts, laid end to end along the dimension named above; an argument that names none is the same for every part. Nothing has to cross between parts.
Inputs may be any that keep to these rules, and one draw needn't show every extreme that they name: `turn_id`: turn ids never fall along the sequence; each turn covers 1 to 12 consecutive blocks, one exactly 12. `ref_flag`: each aligned group of 6 blocks holds at most 2 reference blocks, some group exactly 2.
All inputs are finite; a program needn't handle non-finite values.
Results may differ from the reference program's by a relative error of at most 0.0034.
The reference program's roundings to bfloat16 on the way (of `modded`, `projected`, `weights` and `attended`) count: a program that leaves them out, or rounds other values in their place, can miss the bound.
Values may be sent and summed in bfloat16 or wider, within the bound.
A program may use at most 128 MiB of HBM per device.

```python
import math
import jax
import jax.numpy as jnp
import numpy as np
from jax import lax

D = 1024
HEAD_COUNT = 16
HEAD_DIM = 64
BLOCK = 128
SPEAKERS = 4
REF_DEV = 2
SEQ = 6144
NB = 48
GROUP_BLOCKS = 6
TURN_MAX = 12
N_BLK = 8


def draw_w_qkv(key, part):
    key = jax.random.fold_in(key, 5)
    key_main = jax.random.fold_in(key, 0)
    return jnp.clip(jax.random.normal(key_main, (D, 3 * D), jnp.float32) * D ** (-0.5), -4.0, 4.0).astype(jnp.bfloat16)


def draw_ref_flag(key, part):
    key = jax.random.fold_in(key, 11)
    groups = NB // GROUP_BLOCKS
    key_count, key_full, key_rank = jax.random.split(key, 3)
    counts = jax.random.randint(key_count, (groups,), 0, REF_DEV + 1)
    fullest = jax.random.randint(key_full, (), 0, groups)
    counts = jnp.where(jnp.arange(groups) == fullest, REF_DEV, counts)
    scores = jax.random.randint(key_rank, (groups, GROUP_BLOCKS), 0, 2 ** 20) * GROUP_BLOCKS + jnp.arange(GROUP_BLOCKS)[None, :]
    order = jnp.argsort(scores, axis=1, stable=True)
    ranks = jnp.argsort(order, axis=1, stable=True)
    return (ranks < counts[:, None]).astype(jnp.int32).reshape(NB)


def place_ends(result, stream_key, smallest, top_value):
    longest = result.shape.index(max(result.shape))
    spots = []
    for shift in (0, 1):
        where = [jax.random.randint(jax.random.fold_in(stream_key, axis), (), 0, length) for axis, length in enumerate(result.shape)]
        where[longest] = (where[longest] + shift) % result.shape[longest]
        spots.append(tuple(where))
    return result.at[spots[0]].set(smallest).at[spots[1]].set(top_value)


def steps_of(key, dims, shards, low, largest):
    factor_of, own = 1.0, jax.random.fold_in(key, 6)
    for axis_at, blocks in shards:
        heights = jnp.exp(jax.random.uniform(jax.random.fold_in(own, axis_at), (blocks,), jnp.float32, low / len(shards), largest / len(shards)))
        factor_of = factor_of * jnp.repeat(heights, dims[axis_at] // blocks).reshape([-1 if axis == axis_at else 1 for axis in range(len(dims))])
    return factor_of


def profile(amount, total, most, slope):
    loads = [(1 << 20) // math.isqrt(rank ** slope) + 1 for rank in range(2, amount + 1)]
    spare, given = total - most - (amount - 1), [1] * (amount - 1)
    while spare > 0:
        free = [i for i in range(amount - 1) if given[i] < most]
        mass, budget = sum([loads[i] for i in free]), spare
        for i in free:
            more = min(most - given[i], max(1, budget * loads[i] // mass), spare)
            given[i] = given[i] + more
            spare = spare - more
    return np.array([most] + given)


def ragged(key, number_of, total, most, skew):
    if number_of == 2:
        one = jax.random.randint(key, (), max(1, total - most), min(most, total - 1) + 1)
        return jnp.stack([one, total - one])
    lengths = jnp.asarray(profile(number_of, total, most, skew), jnp.int32)
    pairs = (number_of - 1) // 2
    giver, sink = lengths[1:1 + 2 * pairs:2], lengths[2:2 + 2 * pairs:2]
    margin = jnp.minimum(giver - 1, most - sink)
    passed = jax.random.randint(jax.random.fold_in(key, 1), (pairs,), 0, 1 << 20) % (margin + 1)
    lengths = lengths.at[1:1 + 2 * pairs:2].set(giver - passed).at[2:2 + 2 * pairs:2].set(sink + passed)
    return lengths[jax.random.permutation(jax.random.fold_in(key, 2), number_of)]


def centred(key, dims, spread, bound, cuts=(), held_as=jnp.bfloat16):
    result = spread * jax.random.normal(key, dims, jnp.float32)
    if cuts:
        result = result * steps_of(key, dims, cuts, -0.22, 0.18)
    return jnp.clip(result, -bound, bound).astype(held_as)


def setup_inputs(seed: int = 0, part: int = 0) -> dict:
    key_list = jax.random.split(jax.random.key(seed), 8)
    part_keys = jax.random.split(jax.random.fold_in(key_list[7], part), 8)
    frames = centred(part_keys[0], (SEQ, D), 1.0, 6.0, ((0, 16),))
    modulation = centred(part_keys[1], (3, D), 0.6, 3.0, (), jnp.float32)
    w_qkv = draw_w_qkv(jax.random.fold_in(key_list[7], 71), part)
    w_out = centred(key_list[3], (D, D), D ** -0.5, 0.1875)
    turn_id = jnp.searchsorted(jnp.cumsum(ragged(part_keys[4], NB // 4, NB, TURN_MAX, 1)), jnp.arange(NB), side="right").astype(jnp.int32)
    speaker = place_ends(jax.random.randint(part_keys[5], (NB,), 0, SPEAKERS), jax.random.fold_in(part_keys[5], 1), 0, SPEAKERS - 1).astype(jnp.int32)
    ref_flag = draw_ref_flag(jax.random.fold_in(jax.random.fold_in(key_list[7], part), 71), part)
    return dict(frames=frames, modulation=modulation, w_qkv=w_qkv, w_out=w_out, turn_id=turn_id, speaker=speaker, ref_flag=ref_flag)


norm_eps = 1e-06
neg_big = -1e+30

def reference(frames, modulation, w_qkv, w_out, turn_id, speaker, ref_flag):
    widened = frames.astype(jnp.float32)
    average = lax.optimization_barrier(jnp.mean(widened, axis=1, keepdims=True))
    centered = widened - average
    variance = lax.optimization_barrier(jnp.mean(centered * centered, axis=1, keepdims=True))
    normed = centered * lax.rsqrt(variance + norm_eps)
    modded = (normed * (1.0 + modulation[1]) + modulation[0]).astype(jnp.bfloat16)
    projected = jnp.dot(modded, w_qkv, preferred_element_type=jnp.float32).astype(jnp.bfloat16)
    queries = projected[:, :D].reshape(SEQ, HEAD_COUNT, HEAD_DIM)
    key_rows = projected[:, D:2 * D].reshape(SEQ, HEAD_COUNT, HEAD_DIM)
    values = projected[:, 2 * D:].reshape(SEQ, HEAD_COUNT, HEAD_DIM)
    row_block = jnp.arange(SEQ, dtype=jnp.int32) // BLOCK
    turn_rows = turn_id[row_block]
    speak_rows = speaker[row_block]
    ref_rows = ref_flag[row_block]
    tile_rows = SEQ // N_BLK
    tiles = SEQ // tile_rows
    score_scale = HEAD_DIM ** (-0.5)

    def one_tile(item):
        head = (item // tiles).astype(jnp.int32)
        first_row = (item % tiles * tile_rows).astype(jnp.int32)
        query_head = lax.dynamic_index_in_dim(queries, head, 1, keepdims=False)
        query_tile = lax.dynamic_slice_in_dim(query_head, first_row, tile_rows, 0)
        key_head = lax.dynamic_index_in_dim(key_rows, head, 1, keepdims=False)
        value_head = lax.dynamic_index_in_dim(values, head, 1, keepdims=False)
        scores = jnp.dot(query_tile, key_head.T, preferred_element_type=jnp.float32) * score_scale
        turn_q = lax.dynamic_slice_in_dim(turn_rows, first_row, tile_rows)
        speak_q = lax.dynamic_slice_in_dim(speak_rows, first_row, tile_rows)
        allowed = (turn_q[:, None] == turn_rows[None, :]) | (ref_rows[None, :] == 1) & (speak_q[:, None] == speak_rows[None, :])
        masked = jnp.where(allowed, scores, neg_big)
        row_max = lax.optimization_barrier(jnp.max(masked, axis=1, keepdims=True))
        weights = jnp.where(allowed, jnp.exp(masked - row_max), 0.0)
        denominator = lax.optimization_barrier(jnp.sum(weights, axis=1, keepdims=True))
        return jnp.dot(weights.astype(jnp.bfloat16), value_head, preferred_element_type=jnp.float32) / denominator
    outputs = lax.map(one_tile, jnp.arange(HEAD_COUNT * tiles, dtype=jnp.int32))
    attended = outputs.reshape(HEAD_COUNT, SEQ, HEAD_DIM).transpose(1, 0, 2).reshape(SEQ, D).astype(jnp.bfloat16)
    product = jnp.dot(attended, w_out, preferred_element_type=jnp.float32)
    return (widened + modulation[2] * product).astype(jnp.bfloat16)
```

```python
import jax
import jax.numpy as jnp
from jax import lax
from jax.experimental import pallas as pl
from jax.experimental.pallas import tpu as pltpu
from jax.sharding import PartitionSpec as P

HEAD_DIM = 64
BLOCK = 128
TURN_MAX = 12
REF_DEV = 2
CHUNK = 4

norm_eps = 1e-06
score_factor = HEAD_DIM ** (-0.5) * 1.4426950408889634


def modulate(frames, modulation):
    widened = frames.astype(jnp.float32)
    average = jnp.mean(widened, axis=1, keepdims=True)
    centered = widened - average
    variance = jnp.mean(centered * centered, axis=1, keepdims=True)
    normed = centered * lax.rsqrt(variance + norm_eps)
    return (normed * (1.0 + modulation[1]) + modulation[0]).astype(jnp.bfloat16)


def attend_kernel(
    turn, speaker, ref_flag, own, gathered, w_qkv, w_out, frames, modulation, out,
    need, lists, counts, kv, held, queries, top, total, weighted, attended, sems,
):
    blocks = turn.shape[0]
    width = own.shape[1]
    own_blocks = own.shape[0] // BLOCK
    pairs = width // (2 * HEAD_DIM)
    list_len = lists.shape[0] // own_blocks
    device = lax.axis_index("blk") * lax.axis_size("heads") + lax.axis_index("heads")
    first = device * own_blocks

    def scan_block(b, filled):
        slot, lengths = filled[0], filled[1:]
        used = jnp.int32(0)
        updated = []
        for i in range(own_blocks):
            fits = (turn[b] == turn[first + i]) | (
                (ref_flag[b] == 1) & (speaker[b] == speaker[first + i])
            )
            hit = jnp.where(fits, 1, 0).astype(jnp.int32)
            lists[i * list_len + lengths[i]] = slot
            updated.append(lengths[i] + hit)
            used = used | hit
        need[slot] = b
        return (slot + used, *updated)

    zero = jnp.int32(0)
    filled = lax.fori_loop(0, blocks, scan_block, (zero,) * (own_blocks + 1))
    needed = filled[0]
    for i in range(own_blocks):
        length = filled[1 + i]
        counts[i] = length
        lists[i * list_len + length] = lists[i * list_len + length - 1]
    for extra in range(CHUNK):
        need[needed + extra] = need[needed - 1]
    chunks = (needed + CHUNK - 1) // CHUNK

    def fetch(chunk, side):
        return [
            pltpu.make_async_copy(
                gathered.at[pl.ds(pl.multiple_of(need[chunk * CHUNK + k] * BLOCK, BLOCK), BLOCK)],
                held.at[side, pl.ds(k * BLOCK, BLOCK)],
                sems.at[side, k],
            )
            for k in range(CHUNK)
        ]

    for copy in fetch(0, 0):
        copy.start()

    lane = lax.broadcasted_iota(jnp.int32, (BLOCK, 2 * HEAD_DIM), 1)
    lower = lane < HEAD_DIM
    step = 512
    for col in range(0, width, step):
        part = jnp.dot(
            own[...], w_qkv[:, col : col + step], preferred_element_type=jnp.float32
        ).astype(jnp.bfloat16)
        for i in range(own_blocks):
            for local in range(step // (2 * HEAD_DIM)):
                tile = part[i * BLOCK : (i + 1) * BLOCK, local * 128 : (local + 1) * 128]
                p = col // (2 * HEAD_DIM) + local
                queries[i, p, :BLOCK] = jnp.where(lower, tile, 0).astype(jnp.bfloat16)
                queries[i, p, BLOCK:] = jnp.where(lower, 0, tile).astype(jnp.bfloat16)

    def project(chunk, _):
        side = lax.rem(chunk, 2)

        @pl.when(chunk + 1 < chunks)
        def _():
            for copy in fetch(chunk + 1, 1 - side):
                copy.start()

        for copy in fetch(chunk, side):
            copy.wait()
        rows = held[side]
        for col in range(0, 2 * width, step):
            part = jnp.dot(
                rows, w_qkv[:, width + col : width + col + step],
                preferred_element_type=jnp.float32,
            ).astype(jnp.bfloat16)
            kv[pl.ds(pl.multiple_of(chunk * CHUNK * BLOCK, BLOCK), CHUNK * BLOCK), col : col + step] = part
        return 0

    lax.fori_loop(0, chunks, project, 0)

    def one_query_block(i, _):
        length = counts[i]
        steps = (length + 1) // 2

        def rows_of(t):
            start = lists[i * list_len + t]
            return pl.ds(pl.multiple_of(start * BLOCK, BLOCK), BLOCK)

        def score(p, a, b):
            keys = jnp.concatenate(
                [kv[a, p * 128 : (p + 1) * 128], kv[b, p * 128 : (p + 1) * 128]], axis=0
            )
            return lax.dot_general(
                queries[i, p], keys, (((1,), (1,)), ((), ())), preferred_element_type=jnp.float32
            )

        top[...] = jnp.full(top.shape, -jnp.inf, jnp.float32)

        def find_top(t, _):
            a, b = rows_of(2 * t), rows_of(2 * t + 1)
            for p in range(pairs):
                s = score(p, a, b)
                top[p] = jnp.maximum(top[p], jnp.maximum(s[:, :BLOCK], s[:, BLOCK:]))
            return 0

        lax.fori_loop(0, steps, find_top, 0)
        for p in range(pairs):
            top[p] = jnp.broadcast_to(jnp.max(top[p], axis=1, keepdims=True), top.shape[1:])
        total[...] = jnp.zeros(total.shape, jnp.float32)
        weighted[...] = jnp.zeros(weighted.shape, jnp.float32)

        def add_up(t, _):
            a, b = rows_of(2 * t), rows_of(2 * t + 1)
            drop = jnp.where(2 * t + 1 < length, 0.0, 1e30).astype(jnp.float32)
            for p in range(pairs):
                s = score(p, a, b)
                high = top[p]
                wa = jnp.exp2((s[:, :BLOCK] - high) * score_factor)
                wb = jnp.exp2((s[:, BLOCK:] - (high + drop)) * score_factor)
                total[p] += wa + wb
                values = jnp.concatenate(
                    [
                        kv[a, width + p * 128 : width + (p + 1) * 128],
                        kv[b, width + p * 128 : width + (p + 1) * 128],
                    ],
                    axis=0,
                )
                weights = jnp.concatenate(
                    [wa.astype(jnp.bfloat16), wb.astype(jnp.bfloat16)], axis=1
                )
                weighted[p] += jnp.dot(weights, values, preferred_element_type=jnp.float32)
            return 0

        lax.fori_loop(0, steps, add_up, 0)
        at = pl.ds(pl.multiple_of(i * BLOCK, BLOCK), BLOCK)
        for p in range(pairs):
            ratio = weighted[p] / jnp.sum(total[p], axis=1, keepdims=True)
            attended[at, p * 128 : (p + 1) * 128] = jnp.where(
                lower, ratio[:BLOCK], ratio[BLOCK:]
            ).astype(jnp.bfloat16)
        return 0

    lax.fori_loop(0, own_blocks, one_query_block, 0)

    for col in range(0, width, step):
        product = jnp.dot(
            attended[...], w_out[:, col : col + step], preferred_element_type=jnp.float32
        )
        out[:, col : col + step] = (
            frames[:, col : col + step].astype(jnp.float32)
            + modulation[2:3, col : col + step] * product
        ).astype(jnp.bfloat16)


def attend(own, gathered, w_qkv, w_out, frames, modulation, turn_id, speaker, ref_flag):
    rows, width = frames.shape
    blocks = turn_id.shape[0]
    own_blocks = rows // BLOCK
    groups = lax.axis_size("blk")
    most = min(blocks, own_blocks + 2 * (TURN_MAX - 1) + REF_DEV * groups)
    slots = -(-most // CHUNK) * CHUNK
    list_len = min(blocks, TURN_MAX + REF_DEV * groups) + 4
    pairs = width // (2 * HEAD_DIM)
    smem = pl.BlockSpec(memory_space=pltpu.SMEM)
    vmem = pl.BlockSpec(memory_space=pltpu.VMEM)
    return pl.pallas_call(
        attend_kernel,
        out_shape=jax.ShapeDtypeStruct(frames.shape, jnp.bfloat16),
        in_specs=[smem] * 3 + [vmem, pl.BlockSpec(memory_space=pl.ANY)] + [vmem] * 4,
        out_specs=vmem,
        scratch_shapes=[
            pltpu.SMEM((slots + CHUNK + 4,), jnp.int32),
            pltpu.SMEM((own_blocks * list_len,), jnp.int32),
            pltpu.SMEM((own_blocks,), jnp.int32),
            pltpu.VMEM((slots * BLOCK, 2 * width), jnp.bfloat16),
            pltpu.VMEM((2, CHUNK * BLOCK, width), jnp.bfloat16),
            pltpu.VMEM((own_blocks, pairs, 2 * BLOCK, 2 * HEAD_DIM), jnp.bfloat16),
            pltpu.VMEM((pairs, 2 * BLOCK, BLOCK), jnp.float32),
            pltpu.VMEM((pairs, 2 * BLOCK, BLOCK), jnp.float32),
            pltpu.VMEM((pairs, 2 * BLOCK, 2 * HEAD_DIM), jnp.float32),
            pltpu.VMEM((rows, width), jnp.bfloat16),
            pltpu.SemaphoreType.DMA((2, CHUNK)),
        ],
        compiler_params=pltpu.CompilerParams(vmem_limit_bytes=62 * 1024 * 1024),
        cost_estimate=pl.CostEstimate(
            flops=20_000_000_000, bytes_accessed=20_000_000, transcendentals=10_000_000
        ),
    )(turn_id, speaker, ref_flag, own, gathered, w_qkv, w_out, frames, modulation)


def per_device(frames, modulation, w_qkv, w_out, turn_id, speaker, ref_flag):
    modded = modulate(frames, modulation)
    gathered = lax.all_gather(modded, ("blk", "heads"), axis=0, tiled=True)
    return attend(modded, gathered, w_qkv, w_out, frames, modulation, turn_id, speaker, ref_flag)


def solution(mesh):
    return jax.shard_map(
        per_device,
        mesh=mesh,
        in_specs=(
            P(("parts", "blk", "heads"), None),
            P("parts", None),
            P(),
            P(),
            P("parts"),
            P("parts"),
            P("parts"),
        ),
        out_specs=P(("parts", "blk", "heads"), None),
        check_vma=False,
    )
```

```python
import jax
import jax.numpy as jnp
from jax import lax
from jax.experimental import pallas as pl
from jax.experimental.pallas import tpu as pltpu
from jax.sharding import PartitionSpec as P

HEAD_DIM = 64
BLOCK = 128
TURN_MAX = 12
REF_DEV = 2
CHUNK = 4

norm_eps = 1e-06
score_factor = HEAD_DIM ** (-0.5) * 1.4426950408889634


def modulate(frames, modulation):
    widened = frames.astype(jnp.float32)
    average = jnp.mean(widened, axis=1, keepdims=True)
    centered = widened - average
    variance = jnp.mean(centered * centered, axis=1, keepdims=True)
    normed = centered * lax.rsqrt(variance + norm_eps)
    return (normed * (1.0 + modulation[1]) + modulation[0]).astype(jnp.bfloat16)


def exchange_kernel(
    ref_flag, own, gathered, group, staged, near_sems, near_twin_sems, twin_sems,
    line_sems, mate_sems, far_twin_sems, local_sems,
):
    rows = own.shape[0]
    groups = lax.axis_size("blk")
    cores = lax.axis_size("heads")
    hops = groups // 2 - 1
    blocks = cores * rows // BLOCK
    far_first = 5 * cores * rows
    g = lax.axis_index("blk")
    c = lax.axis_index("heads")
    twin = {"heads": 1 - c}
    mate = g + 1 - 2 * lax.rem(g, 2)

    def inside(q):
        return (q >= 0) & (q < groups)

    def is_far(a, b):
        return (a - b >= 3) | (b - a >= 3)

    def near_at(offset, core):
        start = pl.multiple_of((offset + 2) * cores * rows + core * rows, BLOCK)
        return gathered.at[pl.ds(start, rows)]

    def far_at(source, core):
        start = pl.multiple_of(far_first + (source * cores + core) * BLOCK, BLOCK)
        return gathered.at[pl.ds(start, BLOCK)]

    def remote(src, dst, sems, index, device):
        return pltpu.make_async_remote_copy(
            src_ref=src, dst_ref=dst, send_sem=sems.at[(0, *index)], recv_sem=sems.at[(1, *index)],
            device_id=device, device_id_type=pl.DeviceIdType.MESH,
        )

    def near_send(offset):
        return remote(own, near_at(-offset, c), near_sems, (2 - offset,), {"blk": g + offset})

    def near_twin(offset):
        return remote(near_at(offset, c), near_at(offset, c), near_twin_sems, (2 + offset,), twin)

    def line_send(way, hop, source):
        src = staged if hop == 1 else far_at(source, c)
        return remote(src, far_at(source, c), line_sems, (way, hop), {"blk": g + 2 - 4 * way})

    def mate_send(source):
        return remote(far_at(source, c), far_at(source, c), mate_sems, (source,), {"blk": mate})

    def far_twin(source):
        return remote(far_at(source, c), far_at(source, c), far_twin_sems, (source,), twin)

    offsets = (1, -1, 2, -2)
    barrier = pltpu.get_barrier_semaphore()
    pl.semaphore_signal(barrier, inc=1, device_id=twin, device_id_type=pl.DeviceIdType.MESH)
    for offset in offsets:
        @pl.when(inside(g + offset))
        def _():
            pl.semaphore_signal(
                barrier, inc=1, device_id={"blk": g + offset}, device_id_type=pl.DeviceIdType.MESH
            )
    peers = 1 + sum(jnp.where(inside(g + offset), 1, 0).astype(jnp.int32) for offset in offsets)
    pl.semaphore_wait(barrier, peers)

    to_twin = remote(own, group.at[c], twin_sems, (), twin)
    to_twin.start()
    for offset in offsets:
        @pl.when(inside(g + offset))
        def _():
            near_send(offset).start()
    keep = pltpu.make_async_copy(own, near_at(0, c), local_sems.at[0])
    keep.start()
    mine = pltpu.make_async_copy(own, group.at[c], local_sems.at[1])
    mine.start()
    mine.wait()
    to_twin.wait_recv()
    keep_twin = pltpu.make_async_copy(group.at[1 - c], near_at(0, 1 - c), local_sems.at[2])
    keep_twin.start()

    rank = jnp.int32(0)
    chosen = group[0, :BLOCK]
    for b in range(blocks):
        flag = ref_flag[g * blocks + b]
        first = (b * BLOCK) % rows
        tile = group[(b * BLOCK) // rows, first : first + BLOCK]
        chosen = jnp.where((flag == 1) & (rank == c), tile, chosen)
        rank = rank + flag
    staged[...] = chosen

    def each_line(act):
        for hop in range(1, hops + 1):
            for way in range(2):
                act(hop, way, g - 2 * hop if way == 0 else g + 2 * hop)

    for way in range(2):
        @pl.when(inside(g + 2 - 4 * way))
        def _():
            line_send(way, 1, g).start()

    def pass_on(hop, way, source):
        @pl.when(inside(source))
        def _():
            line_send(way, hop, source).wait_recv()
            if hop < hops:
                @pl.when(inside(g + 2 - 4 * way))
                def _():
                    line_send(way, hop + 1, source).start()

            @pl.when(is_far(source, mate))
            def _():
                mate_send(source).start()

            if hop >= 2:
                far_twin(source).start()

    each_line(pass_on)

    for offset in offsets:
        @pl.when(inside(g + offset))
        def _():
            near_send(-offset).wait_recv()
            near_twin(offset).start()

    def each_mate(act):
        for k in range(-hops, hops + 1):
            source = mate + 2 * k

            @pl.when(inside(source) & is_far(source, g))
            def _():
                act(source)

    def from_mate(source):
        mate_send(source).wait_recv()
        far_twin(source).start()

    each_mate(from_mate)

    def finish_line(hop, way, source):
        @pl.when(inside(source))
        def _():
            if hop < hops:
                @pl.when(inside(g + 2 - 4 * way))
                def _():
                    line_send(way, hop + 1, source).wait_send()

            @pl.when(is_far(source, mate))
            def _():
                mate_send(source).wait_send()

            if hop >= 2:
                far_twin(source).wait()

    for way in range(2):
        @pl.when(inside(g + 2 - 4 * way))
        def _():
            line_send(way, 1, g).wait_send()
    each_line(finish_line)
    each_mate(lambda source: far_twin(source).wait())
    for offset in offsets:
        @pl.when(inside(g + offset))
        def _():
            near_send(offset).wait_send()
            near_twin(offset).wait()
    to_twin.wait_send()
    keep.wait()
    keep_twin.wait()


def exchange(modded, ref_flag):
    rows, width = modded.shape
    groups = lax.axis_size("blk")
    cores = lax.axis_size("heads")
    dma = pltpu.SemaphoreType.DMA
    return pl.pallas_call(
        exchange_kernel,
        out_shape=jax.ShapeDtypeStruct(
            (5 * cores * rows + groups * REF_DEV * BLOCK, width), modded.dtype
        ),
        in_specs=[
            pl.BlockSpec(memory_space=pltpu.SMEM),
            pl.BlockSpec(memory_space=pltpu.VMEM),
        ],
        out_specs=pl.BlockSpec(memory_space=pl.ANY),
        scratch_shapes=[
            pltpu.VMEM((cores, rows, width), modded.dtype),
            pltpu.VMEM((BLOCK, width), modded.dtype),
            dma((2, 5)),
            dma((2, 5)),
            dma((2,)),
            dma((2, 2, groups // 2)),
            dma((2, groups)),
            dma((2, groups)),
            dma((3,)),
        ],
        compiler_params=pltpu.CompilerParams(
            collective_id=0, has_side_effects=True, vmem_limit_bytes=16 * 1024 * 1024
        ),
    )(ref_flag, modded)


def attend_kernel(
    turn, speaker, ref_flag, own, gathered, w_qkv, w_out, frames, modulation, out,
    need, lists, counts, kv, held, queries, top, total, weighted, attended, sems,
):
    blocks = turn.shape[0]
    width = own.shape[1]
    own_blocks = own.shape[0] // BLOCK
    pairs = width // (2 * HEAD_DIM)
    list_len = lists.shape[0] // own_blocks
    cores = lax.axis_size("heads")
    group_blocks = cores * own_blocks
    group = lax.axis_index("blk")
    device = group * cores + lax.axis_index("heads")
    first = device * own_blocks

    def scan_block(b, filled):
        slot, rank, lengths = filled[0], filled[1], filled[2:]
        source = b // group_blocks
        inner = b - source * group_blocks
        rank = jnp.where(inner == 0, 0, rank)
        offset = source - group
        near = (offset >= -2) & (offset <= 2)
        place = jnp.where(
            near, (offset + 2) * group_blocks + inner, 5 * group_blocks + source * REF_DEV + rank
        )
        used = jnp.int32(0)
        updated = []
        for i in range(own_blocks):
            fits = (turn[b] == turn[first + i]) | (
                (ref_flag[b] == 1) & (speaker[b] == speaker[first + i])
            )
            hit = jnp.where(fits, 1, 0).astype(jnp.int32)
            lists[i * list_len + lengths[i]] = slot
            updated.append(lengths[i] + hit)
            used = used | hit
        need[slot] = place
        return (slot + used, rank + ref_flag[b], *updated)

    zero = jnp.int32(0)
    filled = lax.fori_loop(0, blocks, scan_block, (zero,) * (own_blocks + 2))
    needed = filled[0]
    for i in range(own_blocks):
        length = filled[2 + i]
        counts[i] = length
        lists[i * list_len + length] = lists[i * list_len + length - 1]
    for extra in range(CHUNK):
        need[needed + extra] = need[needed - 1]
    chunks = (needed + CHUNK - 1) // CHUNK

    def fetch(chunk, side):
        return [
            pltpu.make_async_copy(
                gathered.at[pl.ds(pl.multiple_of(need[chunk * CHUNK + k] * BLOCK, BLOCK), BLOCK)],
                held.at[side, pl.ds(k * BLOCK, BLOCK)],
                sems.at[side, k],
            )
            for k in range(CHUNK)
        ]

    for copy in fetch(0, 0):
        copy.start()

    lane = lax.broadcasted_iota(jnp.int32, (BLOCK, 2 * HEAD_DIM), 1)
    lower = lane < HEAD_DIM
    step = 512
    for col in range(0, width, step):
        part = jnp.dot(
            own[...], w_qkv[:, col : col + step], preferred_element_type=jnp.float32
        ).astype(jnp.bfloat16)
        for i in range(own_blocks):
            for local in range(step // (2 * HEAD_DIM)):
                tile = part[i * BLOCK : (i + 1) * BLOCK, local * 128 : (local + 1) * 128]
                p = col // (2 * HEAD_DIM) + local
                queries[i, p, :BLOCK] = jnp.where(lower, tile, 0).astype(jnp.bfloat16)
                queries[i, p, BLOCK:] = jnp.where(lower, 0, tile).astype(jnp.bfloat16)

    def project(chunk, _):
        side = lax.rem(chunk, 2)

        @pl.when(chunk + 1 < chunks)
        def _():
            for copy in fetch(chunk + 1, 1 - side):
                copy.start()

        for copy in fetch(chunk, side):
            copy.wait()
        rows = held[side]
        for col in range(0, 2 * width, step):
            part = jnp.dot(
                rows, w_qkv[:, width + col : width + col + step],
                preferred_element_type=jnp.float32,
            ).astype(jnp.bfloat16)
            kv[pl.ds(pl.multiple_of(chunk * CHUNK * BLOCK, BLOCK), CHUNK * BLOCK), col : col + step] = part
        return 0

    lax.fori_loop(0, chunks, project, 0)

    def one_query_block(i, _):
        length = counts[i]
        steps = (length + 1) // 2

        def rows_of(t):
            start = lists[i * list_len + t]
            return pl.ds(pl.multiple_of(start * BLOCK, BLOCK), BLOCK)

        def score(p, a, b):
            keys = jnp.concatenate(
                [kv[a, p * 128 : (p + 1) * 128], kv[b, p * 128 : (p + 1) * 128]], axis=0
            )
            return lax.dot_general(
                queries[i, p], keys, (((1,), (1,)), ((), ())), preferred_element_type=jnp.float32
            )

        top[...] = jnp.full(top.shape, -jnp.inf, jnp.float32)

        def find_top(t, _):
            a, b = rows_of(2 * t), rows_of(2 * t + 1)
            for p in range(pairs):
                s = score(p, a, b)
                top[p] = jnp.maximum(top[p], jnp.maximum(s[:, :BLOCK], s[:, BLOCK:]))
            return 0

        lax.fori_loop(0, steps, find_top, 0)
        for p in range(pairs):
            top[p] = jnp.broadcast_to(jnp.max(top[p], axis=1, keepdims=True), top.shape[1:])
        total[...] = jnp.zeros(total.shape, jnp.float32)
        weighted[...] = jnp.zeros(weighted.shape, jnp.float32)

        def add_up(t, _):
            a, b = rows_of(2 * t), rows_of(2 * t + 1)
            drop = jnp.where(2 * t + 1 < length, 0.0, 1e30).astype(jnp.float32)
            for p in range(pairs):
                s = score(p, a, b)
                high = top[p]
                wa = jnp.exp2((s[:, :BLOCK] - high) * score_factor)
                wb = jnp.exp2((s[:, BLOCK:] - (high + drop)) * score_factor)
                total[p] += wa + wb
                values = jnp.concatenate(
                    [
                        kv[a, width + p * 128 : width + (p + 1) * 128],
                        kv[b, width + p * 128 : width + (p + 1) * 128],
                    ],
                    axis=0,
                )
                weights = jnp.concatenate(
                    [wa.astype(jnp.bfloat16), wb.astype(jnp.bfloat16)], axis=1
                )
                weighted[p] += jnp.dot(weights, values, preferred_element_type=jnp.float32)
            return 0

        lax.fori_loop(0, steps, add_up, 0)
        at = pl.ds(pl.multiple_of(i * BLOCK, BLOCK), BLOCK)
        for p in range(pairs):
            ratio = weighted[p] / jnp.sum(total[p], axis=1, keepdims=True)
            attended[at, p * 128 : (p + 1) * 128] = jnp.where(
                lower, ratio[:BLOCK], ratio[BLOCK:]
            ).astype(jnp.bfloat16)
        return 0

    lax.fori_loop(0, own_blocks, one_query_block, 0)

    for col in range(0, width, step):
        product = jnp.dot(
            attended[...], w_out[:, col : col + step], preferred_element_type=jnp.float32
        )
        out[:, col : col + step] = (
            frames[:, col : col + step].astype(jnp.float32)
            + modulation[2:3, col : col + step] * product
        ).astype(jnp.bfloat16)


def attend(own, gathered, w_qkv, w_out, frames, modulation, turn_id, speaker, ref_flag):
    rows, width = frames.shape
    blocks = turn_id.shape[0]
    own_blocks = rows // BLOCK
    groups = lax.axis_size("blk")
    most = min(blocks, own_blocks + 2 * (TURN_MAX - 1) + REF_DEV * groups)
    slots = -(-most // CHUNK) * CHUNK
    list_len = min(blocks, TURN_MAX + REF_DEV * groups) + 4
    pairs = width // (2 * HEAD_DIM)
    smem = pl.BlockSpec(memory_space=pltpu.SMEM)
    vmem = pl.BlockSpec(memory_space=pltpu.VMEM)
    return pl.pallas_call(
        attend_kernel,
        out_shape=jax.ShapeDtypeStruct(frames.shape, jnp.bfloat16),
        in_specs=[smem] * 3 + [vmem, pl.BlockSpec(memory_space=pl.ANY)] + [vmem] * 4,
        out_specs=vmem,
        scratch_shapes=[
            pltpu.SMEM((slots + CHUNK + 4,), jnp.int32),
            pltpu.SMEM((own_blocks * list_len,), jnp.int32),
            pltpu.SMEM((own_blocks,), jnp.int32),
            pltpu.VMEM((slots * BLOCK, 2 * width), jnp.bfloat16),
            pltpu.VMEM((2, CHUNK * BLOCK, width), jnp.bfloat16),
            pltpu.VMEM((own_blocks, pairs, 2 * BLOCK, 2 * HEAD_DIM), jnp.bfloat16),
            pltpu.VMEM((pairs, 2 * BLOCK, BLOCK), jnp.float32),
            pltpu.VMEM((pairs, 2 * BLOCK, BLOCK), jnp.float32),
            pltpu.VMEM((pairs, 2 * BLOCK, 2 * HEAD_DIM), jnp.float32),
            pltpu.VMEM((rows, width), jnp.bfloat16),
            pltpu.SemaphoreType.DMA((2, CHUNK)),
        ],
        compiler_params=pltpu.CompilerParams(vmem_limit_bytes=62 * 1024 * 1024),
        cost_estimate=pl.CostEstimate(
            flops=20_000_000_000, bytes_accessed=20_000_000, transcendentals=10_000_000
        ),
    )(turn_id, speaker, ref_flag, own, gathered, w_qkv, w_out, frames, modulation)


def per_device(frames, modulation, w_qkv, w_out, turn_id, speaker, ref_flag):
    modded = modulate(frames, modulation)
    gathered = exchange(modded, ref_flag)
    return attend(modded, gathered, w_qkv, w_out, frames, modulation, turn_id, speaker, ref_flag)


def solution(mesh):
    return jax.shard_map(
        per_device,
        mesh=mesh,
        in_specs=(
            P(("parts", "blk", "heads"), None),
            P("parts", None),
            P(),
            P(),
            P("parts"),
            P("parts"),
            P("parts"),
        ),
        out_specs=P(("parts", "blk", "heads"), None),
        check_vma=False,
    )
```

```python
import jax
import jax.numpy as jnp
from jax import lax
from jax.experimental import pallas as pl
from jax.experimental.pallas import tpu as pltpu
from jax.sharding import PartitionSpec as P

HEAD_DIM = 64
BLOCK = 128
TURN_MAX = 12
REF_DEV = 2
CHUNK = 4

norm_eps = 1e-06
score_factor = HEAD_DIM ** (-0.5) * 1.4426950408889634


def modulate(frames, modulation):
    widened = frames.astype(jnp.float32)
    average = jnp.mean(widened, axis=1, keepdims=True)
    centered = widened - average
    variance = jnp.mean(centered * centered, axis=1, keepdims=True)
    normed = centered * lax.rsqrt(variance + norm_eps)
    return (normed * (1.0 + modulation[1]) + modulation[0]).astype(jnp.bfloat16)


def exchange_kernel(
    ref_flag, own, gathered, group, staged, near_sems, near_twin_sems, twin_sems,
    line_sems, mate_sems, far_twin_sems, local_sems,
):
    rows = own.shape[0]
    groups = lax.axis_size("blk")
    cores = lax.axis_size("heads")
    hops = groups // 2 - 1
    blocks = cores * rows // BLOCK
    far_first = 5 * cores * rows
    g = lax.axis_index("blk")
    c = lax.axis_index("heads")
    twin = {"heads": 1 - c}
    mate = g + 1 - 2 * lax.rem(g, 2)

    def inside(q):
        return (q >= 0) & (q < groups)

    def is_far(a, b):
        return (a - b >= 3) | (b - a >= 3)

    def near_at(offset, core):
        start = pl.multiple_of((offset + 2) * cores * rows + core * rows, BLOCK)
        return gathered.at[pl.ds(start, rows)]

    def far_at(source, core):
        start = pl.multiple_of(far_first + (source * cores + core) * BLOCK, BLOCK)
        return gathered.at[pl.ds(start, BLOCK)]

    def remote(src, dst, sems, index, device):
        return pltpu.make_async_remote_copy(
            src_ref=src, dst_ref=dst, send_sem=sems.at[(0, *index)], recv_sem=sems.at[(1, *index)],
            device_id=device, device_id_type=pl.DeviceIdType.MESH,
        )

    def near_send(offset):
        return remote(own, near_at(-offset, c), near_sems, (2 - offset,), {"blk": g + offset})

    def near_twin(offset):
        return remote(near_at(offset, c), near_at(offset, c), near_twin_sems, (2 + offset,), twin)

    def line_send(way, hop, source):
        src = staged if hop == 1 else far_at(source, c)
        return remote(src, far_at(source, c), line_sems, (way, hop), {"blk": g + 2 - 4 * way})

    def mate_send(source):
        return remote(far_at(source, c), far_at(source, c), mate_sems, (source,), {"blk": mate})

    def far_twin(source):
        return remote(far_at(source, c), far_at(source, c), far_twin_sems, (source,), twin)

    offsets = (1, -1, 2, -2)
    barrier = pltpu.get_barrier_semaphore()
    pl.semaphore_signal(barrier, inc=1, device_id=twin, device_id_type=pl.DeviceIdType.MESH)
    for offset in offsets:
        @pl.when(inside(g + offset))
        def _():
            pl.semaphore_signal(
                barrier, inc=1, device_id={"blk": g + offset}, device_id_type=pl.DeviceIdType.MESH
            )
    peers = 1 + sum(jnp.where(inside(g + offset), 1, 0).astype(jnp.int32) for offset in offsets)
    pl.semaphore_wait(barrier, peers)

    to_twin = remote(own, group.at[c], twin_sems, (), twin)
    to_twin.start()
    for offset in offsets:
        @pl.when(inside(g + offset))
        def _():
            near_send(offset).start()
    keep = pltpu.make_async_copy(own, near_at(0, c), local_sems.at[0])
    keep.start()
    mine = pltpu.make_async_copy(own, group.at[c], local_sems.at[1])
    mine.start()
    mine.wait()
    to_twin.wait_recv()
    keep_twin = pltpu.make_async_copy(group.at[1 - c], near_at(0, 1 - c), local_sems.at[2])
    keep_twin.start()

    rank = jnp.int32(0)
    chosen = group[0, :BLOCK]
    for b in range(blocks):
        flag = ref_flag[g * blocks + b]
        first = (b * BLOCK) % rows
        tile = group[(b * BLOCK) // rows, first : first + BLOCK]
        chosen = jnp.where((flag == 1) & (rank == c), tile, chosen)
        rank = rank + flag
    staged[...] = chosen

    def each_line(act):
        for hop in range(1, hops + 1):
            for way in range(2):
                act(hop, way, g - 2 * hop if way == 0 else g + 2 * hop)

    for way in range(2):
        @pl.when(inside(g + 2 - 4 * way))
        def _():
            line_send(way, 1, g).start()

    def pass_on(hop, way, source):
        @pl.when(inside(source))
        def _():
            line_send(way, hop, source).wait_recv()
            if hop < hops:
                @pl.when(inside(g + 2 - 4 * way))
                def _():
                    line_send(way, hop + 1, source).start()

            @pl.when(is_far(source, mate))
            def _():
                mate_send(source).start()

            if hop >= 2:
                far_twin(source).start()

    each_line(pass_on)

    for offset in offsets:
        @pl.when(inside(g + offset))
        def _():
            near_send(-offset).wait_recv()
            near_twin(offset).start()

    def each_mate(act):
        for k in range(-hops, hops + 1):
            source = mate + 2 * k

            @pl.when(inside(source) & is_far(source, g))
            def _():
                act(source)

    def from_mate(source):
        mate_send(source).wait_recv()
        far_twin(source).start()

    each_mate(from_mate)

    def finish_line(hop, way, source):
        @pl.when(inside(source))
        def _():
            if hop < hops:
                @pl.when(inside(g + 2 - 4 * way))
                def _():
                    line_send(way, hop + 1, source).wait_send()

            @pl.when(is_far(source, mate))
            def _():
                mate_send(source).wait_send()

            if hop >= 2:
                far_twin(source).wait()

    for way in range(2):
        @pl.when(inside(g + 2 - 4 * way))
        def _():
            line_send(way, 1, g).wait_send()
    each_line(finish_line)
    each_mate(lambda source: far_twin(source).wait())
    for offset in offsets:
        @pl.when(inside(g + offset))
        def _():
            near_send(offset).wait_send()
            near_twin(offset).wait()
    to_twin.wait_send()
    keep.wait()
    keep_twin.wait()


def exchange(modded, ref_flag):
    rows, width = modded.shape
    groups = lax.axis_size("blk")
    cores = lax.axis_size("heads")
    dma = pltpu.SemaphoreType.DMA
    return pl.pallas_call(
        exchange_kernel,
        out_shape=jax.ShapeDtypeStruct(
            (5 * cores * rows + groups * REF_DEV * BLOCK, width), modded.dtype
        ),
        in_specs=[
            pl.BlockSpec(memory_space=pltpu.SMEM),
            pl.BlockSpec(memory_space=pltpu.VMEM),
        ],
        out_specs=pl.BlockSpec(memory_space=pl.ANY),
        scratch_shapes=[
            pltpu.VMEM((cores, rows, width), modded.dtype),
            pltpu.VMEM((BLOCK, width), modded.dtype),
            dma((2, 5)),
            dma((2, 5)),
            dma((2,)),
            dma((2, 2, groups // 2)),
            dma((2, groups)),
            dma((2, groups)),
            dma((3,)),
        ],
        compiler_params=pltpu.CompilerParams(
            collective_id=0, has_side_effects=True, vmem_limit_bytes=58 * 1024 * 1024
        ),
    )(ref_flag, modded)


def attend_kernel(
    turn, speaker, ref_flag, own, gathered, w_qkv_far, w_out_far, frames, modulation, out,
    need, lists, counts, w_qkv, w_out, kv, held, queries, top, total, weighted, attended,
    head_of, query_size, key_size, sems, weight_sems,
):
    blocks = turn.shape[0]
    width = own.shape[1]
    own_blocks = own.shape[0] // BLOCK
    pairs = width // (2 * HEAD_DIM)
    list_len = lists.shape[0] // own_blocks
    cores = lax.axis_size("heads")
    group_blocks = cores * own_blocks
    group = lax.axis_index("blk")
    device = group * cores + lax.axis_index("heads")
    first = device * own_blocks

    weights_in = [
        pltpu.make_async_copy(
            w_qkv_far.at[:, pl.ds(0, width)], w_qkv.at[:, pl.ds(0, width)], weight_sems.at[0]
        ),
        pltpu.make_async_copy(
            w_qkv_far.at[:, pl.ds(width, 2 * width)],
            w_qkv.at[:, pl.ds(width, 2 * width)],
            weight_sems.at[1],
        ),
        pltpu.make_async_copy(w_out_far, w_out, weight_sems.at[2]),
    ]
    for copy in weights_in:
        copy.start()

    def scan_block(b, filled):
        slot, rank, lengths = filled[0], filled[1], filled[2:]
        source = b // group_blocks
        inner = b - source * group_blocks
        rank = jnp.where(inner == 0, 0, rank)
        offset = source - group
        near = (offset >= -2) & (offset <= 2)
        place = jnp.where(
            near, (offset + 2) * group_blocks + inner, 5 * group_blocks + source * REF_DEV + rank
        )
        used = jnp.int32(0)
        updated = []
        for i in range(own_blocks):
            fits = (turn[b] == turn[first + i]) | (
                (ref_flag[b] == 1) & (speaker[b] == speaker[first + i])
            )
            hit = jnp.where(fits, 1, 0).astype(jnp.int32)
            lists[i * list_len + lengths[i]] = slot
            updated.append(lengths[i] + hit)
            used = used | hit
        need[slot] = place
        return (slot + used, rank + ref_flag[b], *updated)

    zero = jnp.int32(0)
    filled = lax.fori_loop(0, blocks, scan_block, (zero,) * (own_blocks + 2))
    needed = filled[0]
    for i in range(own_blocks):
        length = filled[2 + i]
        counts[i] = length
        lists[i * list_len + length] = lists[i * list_len + length - 1]
    for extra in range(CHUNK):
        need[needed + extra] = need[needed - 1]
    chunks = (needed + CHUNK - 1) // CHUNK

    def fetch(chunk, side):
        return [
            pltpu.make_async_copy(
                gathered.at[pl.ds(pl.multiple_of(need[chunk * CHUNK + k] * BLOCK, BLOCK), BLOCK)],
                held.at[side, pl.ds(k * BLOCK, BLOCK)],
                sems.at[side, k],
            )
            for k in range(CHUNK)
        ]

    for copy in fetch(0, 0):
        copy.start()

    lane = lax.broadcasted_iota(jnp.int32, (BLOCK, 2 * HEAD_DIM), 1)
    lower = lane < HEAD_DIM
    step = 512

    feature = lax.broadcasted_iota(jnp.int32, head_of.shape, 0)
    column = lax.broadcasted_iota(jnp.int32, head_of.shape, 1)
    head_of[...] = jnp.where(feature // HEAD_DIM == column, 1.0, 0.0).astype(jnp.bfloat16)
    query_size[...] = jnp.zeros(query_size.shape, jnp.float32)
    key_size[...] = jnp.zeros(key_size.shape, jnp.float32)

    def largest(part, col):
        sizes = jnp.dot(
            part * part, head_of[col : col + step], preferred_element_type=jnp.float32
        )
        return jnp.max(sizes.reshape(-1, 8, sizes.shape[1]), axis=0)

    weights_in[0].wait()
    for col in range(0, width, step):
        part = jnp.dot(
            own[...], w_qkv[:, col : col + step], preferred_element_type=jnp.float32
        ).astype(jnp.bfloat16)
        query_size[...] = jnp.maximum(query_size[...], largest(part, col))
        for i in range(own_blocks):
            for local in range(step // (2 * HEAD_DIM)):
                tile = part[i * BLOCK : (i + 1) * BLOCK, local * 128 : (local + 1) * 128]
                p = col // (2 * HEAD_DIM) + local
                queries[i, p, :BLOCK] = jnp.where(lower, tile, 0).astype(jnp.bfloat16)
                queries[i, p, BLOCK:] = jnp.where(lower, 0, tile).astype(jnp.bfloat16)

    weights_in[1].wait()

    def project(chunk, _):
        side = lax.rem(chunk, 2)

        @pl.when(chunk + 1 < chunks)
        def _():
            for copy in fetch(chunk + 1, 1 - side):
                copy.start()

        for copy in fetch(chunk, side):
            copy.wait()
        rows = held[side]
        for col in range(0, 2 * width, step):
            part = jnp.dot(
                rows, w_qkv[:, width + col : width + col + step],
                preferred_element_type=jnp.float32,
            ).astype(jnp.bfloat16)
            if col < width:
                key_size[...] = jnp.maximum(key_size[...], largest(part, col))
            kv[pl.ds(pl.multiple_of(chunk * CHUNK * BLOCK, BLOCK), CHUNK * BLOCK), col : col + step] = part
        return 0

    lax.fori_loop(0, chunks, project, 0)

    bound = jnp.max(
        jnp.max(query_size[...], axis=0, keepdims=True)
        * jnp.max(key_size[...], axis=0, keepdims=True)
    )
    plain = bound * 1.1 < (50.0 * HEAD_DIM**0.5) ** 2

    def one_query_block(i, _):
        length = counts[i]

        def rows_of(t):
            start = lists[i * list_len + t]
            return pl.ds(pl.multiple_of(start * BLOCK, BLOCK), BLOCK)

        def side_by_side(rows, col):
            return jnp.concatenate([kv[r, col : col + 128] for r in rows], axis=0)

        def score(p, rows):
            return lax.dot_general(
                queries[i, p], side_by_side(rows, p * 128), (((1,), (1,)), ((), ())),
                preferred_element_type=jnp.float32,
            )

        def add_up(rows, subtract):
            for p in range(pairs):
                s = score(p, rows)
                weights = []
                for k in range(len(rows)):
                    piece = s[:, k * BLOCK : (k + 1) * BLOCK]
                    if subtract:
                        piece = piece - top[p]
                    weights.append(jnp.exp2(piece * score_factor))
                total[p] += sum(weights)
                rounded = jnp.concatenate([w.astype(jnp.bfloat16) for w in weights], axis=1)
                weighted[p] += jnp.dot(
                    rounded, side_by_side(rows, width + p * 128),
                    preferred_element_type=jnp.float32,
                )

        def find_top(t, _):
            rows = rows_of(2 * t), rows_of(2 * t + 1)
            for p in range(pairs):
                s = score(p, rows)
                top[p] = jnp.maximum(top[p], jnp.maximum(s[:, :BLOCK], s[:, BLOCK:]))
            return 0

        def every_key(subtract):
            def two(t, _):
                add_up((rows_of(2 * t), rows_of(2 * t + 1)), subtract)
                return 0

            lax.fori_loop(0, length // 2, two, 0)

            @pl.when(lax.rem(length, 2) == 1)
            def _():
                add_up((rows_of(length - 1),), subtract)

        total[...] = jnp.zeros(total.shape, jnp.float32)
        weighted[...] = jnp.zeros(weighted.shape, jnp.float32)

        @pl.when(plain)
        def _():
            every_key(False)

        @pl.when(jnp.logical_not(plain))
        def _():
            top[...] = jnp.full(top.shape, -jnp.inf, jnp.float32)
            lax.fori_loop(0, (length + 1) // 2, find_top, 0)
            for p in range(pairs):
                top[p] = jnp.broadcast_to(jnp.max(top[p], axis=1, keepdims=True), top.shape[1:])
            every_key(True)

        at = pl.ds(pl.multiple_of(i * BLOCK, BLOCK), BLOCK)
        for p in range(pairs):
            ratio = weighted[p] * (1.0 / jnp.sum(total[p], axis=1, keepdims=True))
            attended[at, p * 128 : (p + 1) * 128] = jnp.where(
                lower, ratio[:BLOCK], ratio[BLOCK:]
            ).astype(jnp.bfloat16)
        return 0

    lax.fori_loop(0, own_blocks, one_query_block, 0)
    weights_in[2].wait()

    for col in range(0, width, step):
        product = jnp.dot(
            attended[...], w_out[:, col : col + step], preferred_element_type=jnp.float32
        )
        out[:, col : col + step] = (
            frames[:, col : col + step].astype(jnp.float32)
            + modulation[2:3, col : col + step] * product
        ).astype(jnp.bfloat16)


def attend(own, gathered, w_qkv, w_out, frames, modulation, turn_id, speaker, ref_flag):
    rows, width = frames.shape
    blocks = turn_id.shape[0]
    own_blocks = rows // BLOCK
    groups = lax.axis_size("blk")
    most = min(blocks, own_blocks + 2 * (TURN_MAX - 1) + REF_DEV * groups)
    slots = -(-most // CHUNK) * CHUNK
    list_len = min(blocks, TURN_MAX + REF_DEV * groups) + 4
    pairs = width // (2 * HEAD_DIM)
    limit = 2 * (w_qkv.size + w_out.size + slots * BLOCK * 2 * width) + 15 * 1024 * 1024
    smem = pl.BlockSpec(memory_space=pltpu.SMEM)
    vmem = pl.BlockSpec(memory_space=pltpu.VMEM)
    return pl.pallas_call(
        attend_kernel,
        out_shape=jax.ShapeDtypeStruct(frames.shape, jnp.bfloat16),
        in_specs=[smem] * 3 + [vmem] + [pl.BlockSpec(memory_space=pl.ANY)] * 3 + [vmem] * 2,
        out_specs=vmem,
        scratch_shapes=[
            pltpu.SMEM((slots + CHUNK + 4,), jnp.int32),
            pltpu.SMEM((own_blocks * list_len,), jnp.int32),
            pltpu.SMEM((own_blocks,), jnp.int32),
            pltpu.VMEM(w_qkv.shape, w_qkv.dtype),
            pltpu.VMEM(w_out.shape, w_out.dtype),
            pltpu.VMEM((slots * BLOCK, 2 * width), jnp.bfloat16),
            pltpu.VMEM((2, CHUNK * BLOCK, width), jnp.bfloat16),
            pltpu.VMEM((own_blocks, pairs, 2 * BLOCK, 2 * HEAD_DIM), jnp.bfloat16),
            pltpu.VMEM((pairs, 2 * BLOCK, BLOCK), jnp.float32),
            pltpu.VMEM((pairs, 2 * BLOCK, BLOCK), jnp.float32),
            pltpu.VMEM((pairs, 2 * BLOCK, 2 * HEAD_DIM), jnp.float32),
            pltpu.VMEM((rows, width), jnp.bfloat16),
            pltpu.VMEM((width, 128), jnp.bfloat16),
            pltpu.VMEM((8, 128), jnp.float32),
            pltpu.VMEM((8, 128), jnp.float32),
            pltpu.SemaphoreType.DMA((2, CHUNK)),
            pltpu.SemaphoreType.DMA((3,)),
        ],
        compiler_params=pltpu.CompilerParams(vmem_limit_bytes=limit),
        cost_estimate=pl.CostEstimate(
            flops=20_000_000_000, bytes_accessed=20_000_000, transcendentals=10_000_000
        ),
    )(turn_id, speaker, ref_flag, own, gathered, w_qkv, w_out, frames, modulation)


def per_device(frames, modulation, w_qkv, w_out, turn_id, speaker, ref_flag):
    modded = modulate(frames, modulation)
    gathered = exchange(modded, ref_flag)
    return attend(modded, gathered, w_qkv, w_out, frames, modulation, turn_id, speaker, ref_flag)


def solution(mesh):
    return jax.shard_map(
        per_device,
        mesh=mesh,
        in_specs=(
            P(("parts", "blk", "heads"), None),
            P("parts", None),
            P(),
            P(),
            P("parts"),
            P("parts"),
            P("parts"),
        ),
        out_specs=P(("parts", "blk", "heads"), None),
        check_vma=False,
    )
```

```python
import jax
import jax.numpy as jnp
from jax import lax
from jax.experimental import pallas as pl
from jax.experimental.pallas import tpu as pltpu
from jax.sharding import PartitionSpec as P

HEAD_DIM = 64
BLOCK = 128
TURN_MAX = 12
REF_DEV = 2
CHUNK = 4

norm_eps = 1e-06
score_factor = HEAD_DIM ** (-0.5) * 1.4426950408889634


def modulate(frames, modulation):
    widened = frames.astype(jnp.float32)
    average = jnp.mean(widened, axis=1, keepdims=True)
    centered = widened - average
    variance = jnp.mean(centered * centered, axis=1, keepdims=True)
    normed = centered * lax.rsqrt(variance + norm_eps)
    return (normed * (1.0 + modulation[1]) + modulation[0]).astype(jnp.bfloat16)


def exchange_kernel(
    ref_flag, own, gathered, group, staged, near_sems, relay_sems, near_twin_sems, twin_sems,
    line_sems, mate_sems, far_twin_sems, local_sems,
):
    rows = own.shape[0]
    groups = lax.axis_size("blk")
    cores = lax.axis_size("heads")
    hops = groups // 2 - 1
    blocks = cores * rows // BLOCK
    far_first = 5 * cores * rows
    g = lax.axis_index("blk")
    c = lax.axis_index("heads")
    twin = {"heads": 1 - c}
    mate = g + 1 - 2 * lax.rem(g, 2)

    def inside(q):
        return (q >= 0) & (q < groups)

    def is_far(a, b):
        return (a - b >= 3) | (b - a >= 3)

    def near_at(offset, core):
        start = pl.multiple_of((offset + 2) * cores * rows + core * rows, BLOCK)
        return gathered.at[pl.ds(start, rows)]

    def far_at(source, core):
        start = pl.multiple_of(far_first + (source * cores + core) * BLOCK, BLOCK)
        return gathered.at[pl.ds(start, BLOCK)]

    def remote(src, dst, sems, index, device):
        return pltpu.make_async_remote_copy(
            src_ref=src, dst_ref=dst, send_sem=sems.at[(0, *index)], recv_sem=sems.at[(1, *index)],
            device_id=device, device_id_type=pl.DeviceIdType.MESH,
        )

    half_rows = rows // 2
    toward = mate - g

    def half_at(offset, core, half):
        start = (offset + 2) * cores * rows + core * rows + half * half_rows
        return gathered.at[pl.ds(pl.multiple_of(start, half_rows), half_rows)]

    def near_send(offset, half):
        return remote(
            own.at[pl.ds(half * half_rows, half_rows)], half_at(-offset, c, half),
            near_sems, (2 - offset, half), {"blk": g + offset},
        )

    def relay(half):
        if half == 0:
            src, seen, device = half_at(2 * toward, c, 0), toward, mate
        else:
            src, seen, device = half_at(toward, c, 1), -toward, g + 2 * toward
        return pltpu.make_async_remote_copy(
            src_ref=src, dst_ref=half_at(seen, c, half), send_sem=relay_sems.at[half],
            recv_sem=near_sems.at[1, 2 + seen, half], device_id={"blk": device},
            device_id_type=pl.DeviceIdType.MESH,
        )

    def near_twin(offset, half):
        ref = half_at(offset, c, half)
        return remote(ref, ref, near_twin_sems, (2 + offset, half), twin)

    def line_send(way, hop, source):
        src = staged if hop == 1 else far_at(source, c)
        return remote(src, far_at(source, c), line_sems, (way, hop), {"blk": g + 2 - 4 * way})

    def mate_send(source):
        return remote(far_at(source, c), far_at(source, c), mate_sems, (source,), {"blk": mate})

    def far_twin(source):
        return remote(far_at(source, c), far_at(source, c), far_twin_sems, (source,), twin)

    sides = (2 * toward, -2 * toward)
    others = (toward, -toward, *sides)
    barrier = pltpu.get_barrier_semaphore()
    pl.semaphore_signal(barrier, inc=1, device_id=twin, device_id_type=pl.DeviceIdType.MESH)
    pl.semaphore_signal(
        barrier, inc=1, device_id={"blk": mate}, device_id_type=pl.DeviceIdType.MESH
    )
    for offset in sides:
        @pl.when(inside(g + offset))
        def _():
            pl.semaphore_signal(
                barrier, inc=1, device_id={"blk": g + offset}, device_id_type=pl.DeviceIdType.MESH
            )
    peers = 2 + sum(jnp.where(inside(g + offset), 1, 0).astype(jnp.int32) for offset in sides)
    pl.semaphore_wait(barrier, peers)

    to_twin = remote(own, group.at[c], twin_sems, (), twin)
    to_twin.start()
    near_send(toward, 1).start()
    for half in range(2):
        for offset in reversed(sides):
            @pl.when(inside(g + offset))
            def _():
                near_send(offset, half).start()
        if half == 0:
            near_send(toward, 0).start()
    keep = pltpu.make_async_copy(own, near_at(0, c), local_sems.at[0])
    keep.start()
    mine = pltpu.make_async_copy(own, group.at[c], local_sems.at[1])
    mine.start()
    mine.wait()
    to_twin.wait_recv()
    keep_twin = pltpu.make_async_copy(group.at[1 - c], near_at(0, 1 - c), local_sems.at[2])
    keep_twin.start()

    rank = jnp.int32(0)
    chosen = group[0, :BLOCK]
    for b in range(blocks):
        flag = ref_flag[g * blocks + b]
        first = (b * BLOCK) % rows
        tile = group[(b * BLOCK) // rows, first : first + BLOCK]
        chosen = jnp.where((flag == 1) & (rank == c), tile, chosen)
        rank = rank + flag
    staged[...] = chosen

    def each_line(act):
        for hop in range(1, hops + 1):
            for way in range(2):
                act(hop, way, g - 2 * hop if way == 0 else g + 2 * hop)

    for way in range(2):
        @pl.when(inside(g + 2 - 4 * way))
        def _():
            line_send(way, 1, g).start()

    def pass_on(hop, way, source):
        @pl.when(inside(source))
        def _():
            line_send(way, hop, source).wait_recv()
            if hop < hops:
                @pl.when(inside(g + 2 - 4 * way))
                def _():
                    line_send(way, hop + 1, source).start()

            @pl.when(is_far(source, mate))
            def _():
                mate_send(source).start()

            if hop >= 2:
                far_twin(source).start()

    def arrive(offset, half):
        near_send(-offset, half).wait_recv()
        near_twin(offset, half).start()

    arrive(toward, 1)

    @pl.when(inside(g + 2 * toward))
    def _():
        relay(1).start()
        arrive(2 * toward, 0)
        relay(0).start()

    each_line(pass_on)
    arrive(toward, 0)

    @pl.when(inside(g + 2 * toward))
    def _():
        arrive(2 * toward, 1)

    @pl.when(inside(g - 2 * toward))
    def _():
        arrive(-2 * toward, 0)
        arrive(-2 * toward, 1)

    def each_mate(act):
        for k in range(-hops, hops + 1):
            source = mate + 2 * k

            @pl.when(inside(source) & is_far(source, g))
            def _():
                act(source)

    def from_mate(source):
        mate_send(source).wait_recv()
        far_twin(source).start()

    each_mate(from_mate)

    @pl.when(inside(g - toward))
    def _():
        arrive(-toward, 0)
        arrive(-toward, 1)

    def finish_line(hop, way, source):
        @pl.when(inside(source))
        def _():
            if hop < hops:
                @pl.when(inside(g + 2 - 4 * way))
                def _():
                    line_send(way, hop + 1, source).wait_send()

            @pl.when(is_far(source, mate))
            def _():
                mate_send(source).wait_send()

            if hop >= 2:
                far_twin(source).wait()

    for way in range(2):
        @pl.when(inside(g + 2 - 4 * way))
        def _():
            line_send(way, 1, g).wait_send()
    each_line(finish_line)
    each_mate(lambda source: far_twin(source).wait())
    for offset in others:
        @pl.when(inside(g + offset))
        def _():
            for half in range(2):
                near_twin(offset, half).wait()

    for half in range(2):
        near_send(toward, half).wait_send()
        for offset in sides:
            @pl.when(inside(g + offset))
            def _():
                near_send(offset, half).wait_send()

        @pl.when(inside(g + 2 * toward))
        def _():
            relay(half).wait_send()
    to_twin.wait_send()
    keep.wait()
    keep_twin.wait()


def exchange(modded, ref_flag):
    rows, width = modded.shape
    groups = lax.axis_size("blk")
    cores = lax.axis_size("heads")
    dma = pltpu.SemaphoreType.DMA
    return pl.pallas_call(
        exchange_kernel,
        out_shape=jax.ShapeDtypeStruct(
            (5 * cores * rows + groups * REF_DEV * BLOCK, width), modded.dtype
        ),
        in_specs=[
            pl.BlockSpec(memory_space=pltpu.SMEM),
            pl.BlockSpec(memory_space=pltpu.VMEM),
        ],
        out_specs=pl.BlockSpec(memory_space=pl.ANY),
        scratch_shapes=[
            pltpu.VMEM((cores, rows, width), modded.dtype),
            pltpu.VMEM((BLOCK, width), modded.dtype),
            dma((2, 5, 2)),
            dma((2,)),
            dma((2, 5, 2)),
            dma((2,)),
            dma((2, 2, groups // 2)),
            dma((2, groups)),
            dma((2, groups)),
            dma((3,)),
        ],
        compiler_params=pltpu.CompilerParams(
            collective_id=0, has_side_effects=True, vmem_limit_bytes=58 * 1024 * 1024
        ),
    )(ref_flag, modded)


def attend_kernel(
    turn, speaker, ref_flag, own, gathered, w_qkv_far, w_out_far, frames, modulation, out,
    need, lists, counts, w_qkv, w_out, kv, held, queries, top, weighted, attended,
    sems, weight_sems,
):
    blocks = turn.shape[0]
    width = own.shape[1]
    own_blocks = own.shape[0] // BLOCK
    pairs = width // (2 * HEAD_DIM)
    list_len = lists.shape[0] // own_blocks
    cores = lax.axis_size("heads")
    group_blocks = cores * own_blocks
    group = lax.axis_index("blk")
    device = group * cores + lax.axis_index("heads")
    first = device * own_blocks

    weights_in = [
        pltpu.make_async_copy(
            w_qkv_far.at[:, pl.ds(0, width)], w_qkv.at[:, pl.ds(0, width)], weight_sems.at[0]
        ),
        pltpu.make_async_copy(
            w_qkv_far.at[:, pl.ds(width, 2 * width)],
            w_qkv.at[:, pl.ds(width, 2 * width)],
            weight_sems.at[1],
        ),
        pltpu.make_async_copy(w_out_far, w_out, weight_sems.at[2]),
    ]
    for copy in weights_in:
        copy.start()

    def scan_block(b, filled):
        slot, rank, lengths = filled[0], filled[1], filled[2:]
        source = b // group_blocks
        inner = b - source * group_blocks
        rank = jnp.where(inner == 0, 0, rank)
        offset = source - group
        near = (offset >= -2) & (offset <= 2)
        place = jnp.where(
            near, (offset + 2) * group_blocks + inner, 5 * group_blocks + source * REF_DEV + rank
        )
        used = jnp.int32(0)
        updated = []
        for i in range(own_blocks):
            fits = (turn[b] == turn[first + i]) | (
                (ref_flag[b] == 1) & (speaker[b] == speaker[first + i])
            )
            hit = jnp.where(fits, 1, 0).astype(jnp.int32)
            lists[i * list_len + lengths[i]] = slot
            updated.append(lengths[i] + hit)
            used = used | hit
        need[slot] = place
        return (slot + used, rank + ref_flag[b], *updated)

    zero = jnp.int32(0)
    filled = lax.fori_loop(0, blocks, scan_block, (zero,) * (own_blocks + 2))
    needed = filled[0]
    for i in range(own_blocks):
        length = filled[2 + i]
        counts[i] = length
        lists[i * list_len + length] = lists[i * list_len + length - 1]
    for extra in range(CHUNK):
        need[needed + extra] = need[needed - 1]
    chunks = (needed + CHUNK - 1) // CHUNK

    def fetch(chunk, side):
        return [
            pltpu.make_async_copy(
                gathered.at[pl.ds(pl.multiple_of(need[chunk * CHUNK + k] * BLOCK, BLOCK), BLOCK)],
                held.at[side, pl.ds(k * BLOCK, BLOCK)],
                sems.at[side, k],
            )
            for k in range(CHUNK)
        ]

    for copy in fetch(0, 0):
        copy.start()

    lane = lax.broadcasted_iota(jnp.int32, (BLOCK, 2 * HEAD_DIM), 1)
    lower = lane < HEAD_DIM
    step = 512

    weights_in[0].wait()
    for col in range(0, width, step):
        part = jnp.dot(
            own[...], w_qkv[:, col : col + step], preferred_element_type=jnp.float32
        ).astype(jnp.bfloat16)
        for i in range(own_blocks):
            for local in range(step // (2 * HEAD_DIM)):
                tile = part[i * BLOCK : (i + 1) * BLOCK, local * 128 : (local + 1) * 128]
                p = col // (2 * HEAD_DIM) + local
                queries[i, p, :BLOCK] = jnp.where(lower, tile, 0).astype(jnp.bfloat16)
                queries[i, p, BLOCK:] = jnp.where(lower, 0, tile).astype(jnp.bfloat16)

    weights_in[1].wait()

    def project(chunk, _):
        side = lax.rem(chunk, 2)

        @pl.when(chunk + 1 < chunks)
        def _():
            for copy in fetch(chunk + 1, 1 - side):
                copy.start()

        for copy in fetch(chunk, side):
            copy.wait()
        rows = held[side]
        for col in range(0, 2 * width, step):
            part = jnp.dot(
                rows, w_qkv[:, width + col : width + col + step],
                preferred_element_type=jnp.float32,
            ).astype(jnp.bfloat16)
            kv[pl.ds(pl.multiple_of(chunk * CHUNK * BLOCK, BLOCK), CHUNK * BLOCK), col : col + step] = part
        return 0

    lax.fori_loop(0, chunks, project, 0)

    ones = jnp.ones((2 * BLOCK, 128), jnp.bfloat16)

    def one_query_block(i, _):
        length = counts[i]

        def rows_of(t):
            start = lists[i * list_len + t]
            return pl.ds(pl.multiple_of(start * BLOCK, BLOCK), BLOCK)

        def side_by_side(rows, col):
            return jnp.concatenate([kv[r, col : col + 128] for r in rows], axis=0)

        def score(p, rows):
            return lax.dot_general(
                queries[i, p], side_by_side(rows, p * 128), (((1,), (1,)), ((), ())),
                preferred_element_type=jnp.float32,
            )

        def add_up(rows):
            for p in range(pairs):
                s = score(p, rows)
                weights = [
                    jnp.exp2((s[:, k * BLOCK : (k + 1) * BLOCK] - top[p]) * score_factor)
                    for k in range(len(rows))
                ]
                rounded = jnp.concatenate([w.astype(jnp.bfloat16) for w in weights], axis=1)
                values = jnp.concatenate(
                    [side_by_side(rows, width + p * 128), ones[: len(rows) * BLOCK]], axis=1
                )
                weighted[p] += jnp.dot(rounded, values, preferred_element_type=jnp.float32)

        def find_top(t, _):
            rows = rows_of(2 * t), rows_of(2 * t + 1)
            for p in range(pairs):
                s = score(p, rows)
                top[p] = jnp.maximum(top[p], jnp.maximum(s[:, :BLOCK], s[:, BLOCK:]))
            return 0

        def two(t, _):
            add_up((rows_of(2 * t), rows_of(2 * t + 1)))
            return 0

        weighted[...] = jnp.zeros(weighted.shape, jnp.float32)
        top[...] = jnp.full(top.shape, -jnp.inf, jnp.float32)
        lax.fori_loop(0, (length + 1) // 2, find_top, 0)
        for p in range(pairs):
            top[p] = jnp.broadcast_to(jnp.max(top[p], axis=1, keepdims=True), top.shape[1:])
        lax.fori_loop(0, length // 2, two, 0)

        @pl.when(lax.rem(length, 2) == 1)
        def _():
            add_up((rows_of(length - 1),))

        at = pl.ds(pl.multiple_of(i * BLOCK, BLOCK), BLOCK)
        for p in range(pairs):
            ratio = weighted[p, :, :128] / weighted[p, :, 128:]
            attended[at, p * 128 : (p + 1) * 128] = jnp.where(
                lower, ratio[:BLOCK], ratio[BLOCK:]
            ).astype(jnp.bfloat16)
        return 0

    lax.fori_loop(0, own_blocks, one_query_block, 0)
    weights_in[2].wait()

    for col in range(0, width, step):
        product = jnp.dot(
            attended[...], w_out[:, col : col + step], preferred_element_type=jnp.float32
        )
        out[:, col : col + step] = (
            frames[:, col : col + step].astype(jnp.float32)
            + modulation[2:3, col : col + step] * product
        ).astype(jnp.bfloat16)


def attend(own, gathered, w_qkv, w_out, frames, modulation, turn_id, speaker, ref_flag):
    rows, width = frames.shape
    blocks = turn_id.shape[0]
    own_blocks = rows // BLOCK
    groups = lax.axis_size("blk")
    most = min(blocks, own_blocks + 2 * (TURN_MAX - 1) + REF_DEV * groups)
    slots = -(-most // CHUNK) * CHUNK
    list_len = min(blocks, TURN_MAX + REF_DEV * groups) + 4
    pairs = width // (2 * HEAD_DIM)
    limit = 2 * (w_qkv.size + w_out.size + slots * BLOCK * 2 * width) + 15 * 1024 * 1024
    smem = pl.BlockSpec(memory_space=pltpu.SMEM)
    vmem = pl.BlockSpec(memory_space=pltpu.VMEM)
    return pl.pallas_call(
        attend_kernel,
        out_shape=jax.ShapeDtypeStruct(frames.shape, jnp.bfloat16),
        in_specs=[smem] * 3 + [vmem] + [pl.BlockSpec(memory_space=pl.ANY)] * 3 + [vmem] * 2,
        out_specs=vmem,
        scratch_shapes=[
            pltpu.SMEM((slots + CHUNK + 4,), jnp.int32),
            pltpu.SMEM((own_blocks * list_len,), jnp.int32),
            pltpu.SMEM((own_blocks,), jnp.int32),
            pltpu.VMEM(w_qkv.shape, w_qkv.dtype),
            pltpu.VMEM(w_out.shape, w_out.dtype),
            pltpu.VMEM((slots * BLOCK, 2 * width), jnp.bfloat16),
            pltpu.VMEM((2, CHUNK * BLOCK, width), jnp.bfloat16),
            pltpu.VMEM((own_blocks, pairs, 2 * BLOCK, 2 * HEAD_DIM), jnp.bfloat16),
            pltpu.VMEM((pairs, 2 * BLOCK, BLOCK), jnp.float32),
            pltpu.VMEM((pairs, 2 * BLOCK, 4 * HEAD_DIM), jnp.float32),
            pltpu.VMEM((rows, width), jnp.bfloat16),
            pltpu.SemaphoreType.DMA((2, CHUNK)),
            pltpu.SemaphoreType.DMA((3,)),
        ],
        compiler_params=pltpu.CompilerParams(vmem_limit_bytes=limit),
        cost_estimate=pl.CostEstimate(
            flops=20_000_000_000, bytes_accessed=20_000_000, transcendentals=10_000_000
        ),
    )(turn_id, speaker, ref_flag, own, gathered, w_qkv, w_out, frames, modulation)


def per_device(frames, modulation, w_qkv, w_out, turn_id, speaker, ref_flag):
    modded = modulate(frames, modulation)
    gathered = exchange(modded, ref_flag)
    return attend(modded, gathered, w_qkv, w_out, frames, modulation, turn_id, speaker, ref_flag)


def solution(mesh):
    return jax.shard_map(
        per_device,
        mesh=mesh,
        in_specs=(
            P(("parts", "blk", "heads"), None),
            P("parts", None),
            P(),
            P(),
            P("parts"),
            P("parts"),
            P("parts"),
        ),
        out_specs=P(("parts", "blk", "heads"), None),
        check_vma=False,
    )
```

```python
import jax
import jax.numpy as jnp
from jax import lax
from jax.experimental import pallas as pl
from jax.experimental.pallas import tpu as pltpu
from jax.sharding import PartitionSpec as P

HEAD_DIM = 64
BLOCK = 128
TURN_MAX = 12
REF_DEV = 2
CHUNK = 4
WIDE = 4

norm_eps = 1e-06
score_factor = HEAD_DIM ** (-0.5) * 1.4426950408889634


def modulate_kernel(frames, modulation, modded):
    step = BLOCK // 2

    def some_rows(r, _):
        at = pl.ds(pl.multiple_of(r * step, step), step)
        widened = frames[at].astype(jnp.float32)
        average = jnp.mean(widened, axis=1, keepdims=True)
        centered = widened - average
        variance = jnp.mean(centered * centered, axis=1, keepdims=True)
        normed = centered * lax.rsqrt(variance + norm_eps)
        modded[at] = (normed * (1.0 + modulation[1:2]) + modulation[0:1]).astype(jnp.bfloat16)
        return 0

    lax.fori_loop(0, frames.shape[0] // step, some_rows, 0)


def modulate(frames, modulation):
    vmem = pl.BlockSpec(memory_space=pltpu.VMEM)
    return pl.pallas_call(
        modulate_kernel,
        out_shape=jax.ShapeDtypeStruct(frames.shape, jnp.bfloat16),
        in_specs=[vmem, vmem],
        out_specs=vmem,
    )(frames, modulation)


def exchange_kernel(
    ref_flag, own, gathered, group, staged, near_sems, relay_sems, near_twin_sems, twin_sems,
    line_sems, mate_sems, far_twin_sems, local_sems,
):
    rows = own.shape[0]
    groups = lax.axis_size("blk")
    cores = lax.axis_size("heads")
    hops = groups // 2 - 1
    blocks = cores * rows // BLOCK
    far_first = 5 * cores * rows
    g = lax.axis_index("blk")
    c = lax.axis_index("heads")
    twin = {"heads": 1 - c}
    mate = g + 1 - 2 * lax.rem(g, 2)

    def inside(q):
        return (q >= 0) & (q < groups)

    def is_far(a, b):
        return (a - b >= 3) | (b - a >= 3)

    def near_at(offset, core):
        start = pl.multiple_of((offset + 2) * cores * rows + core * rows, BLOCK)
        return gathered.at[pl.ds(start, rows)]

    def far_at(source, core):
        start = pl.multiple_of(far_first + (source * cores + core) * BLOCK, BLOCK)
        return gathered.at[pl.ds(start, BLOCK)]

    def remote(src, dst, sems, index, device):
        return pltpu.make_async_remote_copy(
            src_ref=src, dst_ref=dst, send_sem=sems.at[(0, *index)], recv_sem=sems.at[(1, *index)],
            device_id=device, device_id_type=pl.DeviceIdType.MESH,
        )

    half_rows = rows // 2
    toward = mate - g

    def half_at(offset, core, half):
        start = (offset + 2) * cores * rows + core * rows + half * half_rows
        return gathered.at[pl.ds(pl.multiple_of(start, half_rows), half_rows)]

    def near_send(offset, half):
        return remote(
            own.at[pl.ds(half * half_rows, half_rows)], half_at(-offset, c, half),
            near_sems, (2 - offset, half), {"blk": g + offset},
        )

    def relay(half):
        if half == 0:
            src, seen, device = half_at(2 * toward, c, 0), toward, mate
        else:
            src, seen, device = half_at(toward, c, 1), -toward, g + 2 * toward
        return pltpu.make_async_remote_copy(
            src_ref=src, dst_ref=half_at(seen, c, half), send_sem=relay_sems.at[half],
            recv_sem=near_sems.at[1, 2 + seen, half], device_id={"blk": device},
            device_id_type=pl.DeviceIdType.MESH,
        )

    def near_twin(offset, half):
        ref = half_at(offset, c, half)
        return remote(ref, ref, near_twin_sems, (2 + offset, half), twin)

    def line_send(way, hop, source):
        src = staged if hop == 1 else far_at(source, c)
        return remote(src, far_at(source, c), line_sems, (way, hop), {"blk": g + 2 - 4 * way})

    def mate_send(source):
        return remote(far_at(source, c), far_at(source, c), mate_sems, (source,), {"blk": mate})

    def far_twin(source):
        return remote(far_at(source, c), far_at(source, c), far_twin_sems, (source,), twin)

    sides = (2 * toward, -2 * toward)
    others = (toward, -toward, *sides)
    barrier = pltpu.get_barrier_semaphore()
    pl.semaphore_signal(barrier, inc=1, device_id=twin, device_id_type=pl.DeviceIdType.MESH)
    pl.semaphore_signal(
        barrier, inc=1, device_id={"blk": mate}, device_id_type=pl.DeviceIdType.MESH
    )
    for offset in sides:
        @pl.when(inside(g + offset))
        def _():
            pl.semaphore_signal(
                barrier, inc=1, device_id={"blk": g + offset}, device_id_type=pl.DeviceIdType.MESH
            )
    peers = 2 + sum(jnp.where(inside(g + offset), 1, 0).astype(jnp.int32) for offset in sides)
    pl.semaphore_wait(barrier, peers)

    to_twin = remote(own, group.at[c], twin_sems, (), twin)
    to_twin.start()
    near_send(toward, 1).start()
    for half in range(2):
        for offset in reversed(sides):
            @pl.when(inside(g + offset))
            def _():
                near_send(offset, half).start()
        if half == 0:
            near_send(toward, 0).start()
    keep = pltpu.make_async_copy(own, near_at(0, c), local_sems.at[0])
    keep.start()
    mine = pltpu.make_async_copy(own, group.at[c], local_sems.at[1])
    mine.start()
    mine.wait()
    to_twin.wait_recv()
    keep_twin = pltpu.make_async_copy(group.at[1 - c], near_at(0, 1 - c), local_sems.at[2])
    keep_twin.start()

    rank = jnp.int32(0)
    chosen = group[0, :BLOCK]
    for b in range(blocks):
        flag = ref_flag[g * blocks + b]
        first = (b * BLOCK) % rows
        tile = group[(b * BLOCK) // rows, first : first + BLOCK]
        chosen = jnp.where((flag == 1) & (rank == c), tile, chosen)
        rank = rank + flag
    staged[...] = chosen

    def each_line(act):
        for hop in range(1, hops + 1):
            for way in range(2):
                act(hop, way, g - 2 * hop if way == 0 else g + 2 * hop)

    for way in range(2):
        @pl.when(inside(g + 2 - 4 * way))
        def _():
            line_send(way, 1, g).start()

    def pass_on(hop, way, source):
        @pl.when(inside(source))
        def _():
            line_send(way, hop, source).wait_recv()
            if hop < hops:
                @pl.when(inside(g + 2 - 4 * way))
                def _():
                    line_send(way, hop + 1, source).start()

            @pl.when(is_far(source, mate))
            def _():
                mate_send(source).start()

            if hop >= 2:
                far_twin(source).start()

    def arrive(offset, half):
        near_send(-offset, half).wait_recv()
        near_twin(offset, half).start()

    arrive(toward, 1)

    @pl.when(inside(g + 2 * toward))
    def _():
        relay(1).start()
        arrive(2 * toward, 0)
        relay(0).start()

    each_line(pass_on)
    arrive(toward, 0)

    @pl.when(inside(g + 2 * toward))
    def _():
        arrive(2 * toward, 1)

    @pl.when(inside(g - 2 * toward))
    def _():
        arrive(-2 * toward, 0)
        arrive(-2 * toward, 1)

    def each_mate(act):
        for k in range(-hops, hops + 1):
            source = mate + 2 * k

            @pl.when(inside(source) & is_far(source, g))
            def _():
                act(source)

    def from_mate(source):
        mate_send(source).wait_recv()
        far_twin(source).start()

    each_mate(from_mate)

    @pl.when(inside(g - toward))
    def _():
        arrive(-toward, 0)
        arrive(-toward, 1)

    def finish_line(hop, way, source):
        @pl.when(inside(source))
        def _():
            if hop < hops:
                @pl.when(inside(g + 2 - 4 * way))
                def _():
                    line_send(way, hop + 1, source).wait_send()

            @pl.when(is_far(source, mate))
            def _():
                mate_send(source).wait_send()

            if hop >= 2:
                far_twin(source).wait()

    for way in range(2):
        @pl.when(inside(g + 2 - 4 * way))
        def _():
            line_send(way, 1, g).wait_send()
    each_line(finish_line)
    each_mate(lambda source: far_twin(source).wait())
    for offset in others:
        @pl.when(inside(g + offset))
        def _():
            for half in range(2):
                near_twin(offset, half).wait()

    for half in range(2):
        near_send(toward, half).wait_send()
        for offset in sides:
            @pl.when(inside(g + offset))
            def _():
                near_send(offset, half).wait_send()

        @pl.when(inside(g + 2 * toward))
        def _():
            relay(half).wait_send()
    to_twin.wait_send()
    keep.wait()
    keep_twin.wait()


def exchange(modded, ref_flag):
    rows, width = modded.shape
    groups = lax.axis_size("blk")
    cores = lax.axis_size("heads")
    dma = pltpu.SemaphoreType.DMA
    return pl.pallas_call(
        exchange_kernel,
        out_shape=jax.ShapeDtypeStruct(
            (5 * cores * rows + groups * REF_DEV * BLOCK, width), modded.dtype
        ),
        in_specs=[
            pl.BlockSpec(memory_space=pltpu.SMEM),
            pl.BlockSpec(memory_space=pltpu.VMEM),
        ],
        out_specs=pl.BlockSpec(memory_space=pl.ANY),
        scratch_shapes=[
            pltpu.VMEM((cores, rows, width), modded.dtype),
            pltpu.VMEM((BLOCK, width), modded.dtype),
            dma((2, 5, 2)),
            dma((2,)),
            dma((2, 5, 2)),
            dma((2,)),
            dma((2, 2, groups // 2)),
            dma((2, groups)),
            dma((2, groups)),
            dma((3,)),
        ],
        compiler_params=pltpu.CompilerParams(
            collective_id=0, has_side_effects=True, vmem_limit_bytes=58 * 1024 * 1024
        ),
    )(ref_flag, modded)


def attend_kernel(
    turn, speaker, ref_flag, own, gathered, w_qkv_far, w_out_far, frames, modulation, out,
    need, lists, counts, w_qkv, w_out, kv, held, queries, top, weighted, attended,
    sems, weight_sems,
):
    blocks = turn.shape[0]
    width = own.shape[1]
    own_blocks = own.shape[0] // BLOCK
    pairs = width // (2 * HEAD_DIM)
    list_len = lists.shape[0] // own_blocks
    cores = lax.axis_size("heads")
    group_blocks = cores * own_blocks
    group = lax.axis_index("blk")
    device = group * cores + lax.axis_index("heads")
    first = device * own_blocks

    weights_in = [
        pltpu.make_async_copy(
            w_qkv_far.at[:, pl.ds(0, width)], w_qkv.at[:, pl.ds(0, width)], weight_sems.at[0]
        ),
        pltpu.make_async_copy(
            w_qkv_far.at[:, pl.ds(width, 2 * width)],
            w_qkv.at[:, pl.ds(width, 2 * width)],
            weight_sems.at[1],
        ),
        pltpu.make_async_copy(w_out_far, w_out, weight_sems.at[2]),
    ]
    for copy in weights_in:
        copy.start()

    def scan_block(b, filled):
        slot, rank, lengths = filled[0], filled[1], filled[2:]
        source = b // group_blocks
        inner = b - source * group_blocks
        rank = jnp.where(inner == 0, 0, rank)
        offset = source - group
        near = (offset >= -2) & (offset <= 2)
        place = jnp.where(
            near, (offset + 2) * group_blocks + inner, 5 * group_blocks + source * REF_DEV + rank
        )
        used = jnp.int32(0)
        updated = []
        for i in range(own_blocks):
            fits = (turn[b] == turn[first + i]) | (
                (ref_flag[b] == 1) & (speaker[b] == speaker[first + i])
            )
            hit = jnp.where(fits, 1, 0).astype(jnp.int32)
            lists[i * list_len + lengths[i]] = slot
            updated.append(lengths[i] + hit)
            used = used | hit
        need[slot] = place
        return (slot + used, rank + ref_flag[b], *updated)

    zero = jnp.int32(0)
    filled = lax.fori_loop(0, blocks, scan_block, (zero,) * (own_blocks + 2))
    needed = filled[0]
    for i in range(own_blocks):
        length = filled[2 + i]
        counts[i] = length
        lists[i * list_len + length] = lists[i * list_len + length - 1]
    for extra in range(CHUNK):
        need[needed + extra] = need[needed - 1]
    chunks = (needed + CHUNK - 1) // CHUNK

    def fetch(chunk, side):
        return [
            pltpu.make_async_copy(
                gathered.at[pl.ds(pl.multiple_of(need[chunk * CHUNK + k] * BLOCK, BLOCK), BLOCK)],
                held.at[side, pl.ds(k * BLOCK, BLOCK)],
                sems.at[side, k],
            )
            for k in range(CHUNK)
        ]

    for copy in fetch(0, 0):
        copy.start()

    lane = lax.broadcasted_iota(jnp.int32, (BLOCK, 2 * HEAD_DIM), 1)
    lower = lane < HEAD_DIM
    step = 512

    weights_in[0].wait()
    for col in range(0, width, step):
        part = jnp.dot(
            own[...], w_qkv[:, col : col + step], preferred_element_type=jnp.float32
        ).astype(jnp.bfloat16)
        for i in range(own_blocks):
            for local in range(step // (2 * HEAD_DIM)):
                tile = part[i * BLOCK : (i + 1) * BLOCK, local * 128 : (local + 1) * 128]
                p = col // (2 * HEAD_DIM) + local
                queries[i, p, :BLOCK] = jnp.where(lower, tile, 0).astype(jnp.bfloat16)
                queries[i, p, BLOCK:] = jnp.where(lower, 0, tile).astype(jnp.bfloat16)

    weights_in[1].wait()

    def project(chunk, _):
        side = lax.rem(chunk, 2)

        @pl.when(chunk + 1 < chunks)
        def _():
            for copy in fetch(chunk + 1, 1 - side):
                copy.start()

        for copy in fetch(chunk, side):
            copy.wait()
        rows = held[side]
        for col in range(0, 2 * width, step):
            part = jnp.dot(
                rows, w_qkv[:, width + col : width + col + step],
                preferred_element_type=jnp.float32,
            ).astype(jnp.bfloat16)
            kv[pl.ds(pl.multiple_of(chunk * CHUNK * BLOCK, BLOCK), CHUNK * BLOCK), col : col + step] = part
        return 0

    lax.fori_loop(0, chunks, project, 0)

    ones = jnp.ones((WIDE * BLOCK, 128), jnp.bfloat16)

    def one_query_block(i, _):
        length = counts[i]

        def rows_of(t):
            start = lists[i * list_len + t]
            return pl.ds(pl.multiple_of(start * BLOCK, BLOCK), BLOCK)

        def side_by_side(rows, col):
            return jnp.concatenate([kv[r, col : col + 128] for r in rows], axis=0)

        def score(p, rows):
            return lax.dot_general(
                queries[i, p], side_by_side(rows, p * 128), (((1,), (1,)), ((), ())),
                preferred_element_type=jnp.float32,
            )

        def add_up(rows):
            for p in range(pairs):
                s = score(p, rows)
                weights = [
                    jnp.exp2((s[:, k * BLOCK : (k + 1) * BLOCK] - top[p]) * score_factor)
                    for k in range(len(rows))
                ]
                rounded = jnp.concatenate([w.astype(jnp.bfloat16) for w in weights], axis=1)
                values = jnp.concatenate(
                    [side_by_side(rows, width + p * 128), ones[: len(rows) * BLOCK]], axis=1
                )
                weighted[p] += jnp.dot(rounded, values, preferred_element_type=jnp.float32)

        def find_top(t, _):
            rows = [rows_of(jnp.minimum(WIDE * t + k, length - 1)) for k in range(WIDE)]
            for p in range(pairs):
                s = score(p, rows)
                high = top[p]
                for k in range(WIDE):
                    high = jnp.maximum(high, s[:, k * BLOCK : (k + 1) * BLOCK])
                top[p] = high
            return 0

        def several(t, _):
            add_up([rows_of(WIDE * t + k) for k in range(WIDE)])
            return 0

        weighted[...] = jnp.zeros(weighted.shape, jnp.float32)
        top[...] = jnp.full(top.shape, -jnp.inf, jnp.float32)
        lax.fori_loop(0, (length + WIDE - 1) // WIDE, find_top, 0)
        for p in range(pairs):
            top[p] = jnp.broadcast_to(jnp.max(top[p], axis=1, keepdims=True), top.shape[1:])
        whole = length // WIDE
        lax.fori_loop(0, whole, several, 0)
        left = length - whole * WIDE

        for rest in range(1, WIDE):
            @pl.when(left == rest)
            def _():
                add_up([rows_of(whole * WIDE + k) for k in range(rest)])

        at = pl.ds(pl.multiple_of(i * BLOCK, BLOCK), BLOCK)
        for p in range(pairs):
            ratio = weighted[p, :, :128] / weighted[p, :, 128:]
            attended[at, p * 128 : (p + 1) * 128] = jnp.where(
                lower, ratio[:BLOCK], ratio[BLOCK:]
            ).astype(jnp.bfloat16)
        return 0

    lax.fori_loop(0, own_blocks, one_query_block, 0)
    weights_in[2].wait()

    for col in range(0, width, step):
        product = jnp.dot(
            attended[...], w_out[:, col : col + step], preferred_element_type=jnp.float32
        )
        out[:, col : col + step] = (
            frames[:, col : col + step].astype(jnp.float32)
            + modulation[2:3, col : col + step] * product
        ).astype(jnp.bfloat16)


def attend(own, gathered, w_qkv, w_out, frames, modulation, turn_id, speaker, ref_flag):
    rows, width = frames.shape
    blocks = turn_id.shape[0]
    own_blocks = rows // BLOCK
    groups = lax.axis_size("blk")
    most = min(blocks, own_blocks + 2 * (TURN_MAX - 1) + REF_DEV * groups)
    slots = -(-most // CHUNK) * CHUNK
    list_len = min(blocks, TURN_MAX + REF_DEV * groups) + 4
    pairs = width // (2 * HEAD_DIM)
    limit = 2 * (w_qkv.size + w_out.size + slots * BLOCK * 2 * width) + 15 * 1024 * 1024
    smem = pl.BlockSpec(memory_space=pltpu.SMEM)
    vmem = pl.BlockSpec(memory_space=pltpu.VMEM)
    return pl.pallas_call(
        attend_kernel,
        out_shape=jax.ShapeDtypeStruct(frames.shape, jnp.bfloat16),
        in_specs=[smem] * 3 + [vmem] + [pl.BlockSpec(memory_space=pl.ANY)] * 3 + [vmem] * 2,
        out_specs=vmem,
        scratch_shapes=[
            pltpu.SMEM((slots + CHUNK + 4,), jnp.int32),
            pltpu.SMEM((own_blocks * list_len,), jnp.int32),
            pltpu.SMEM((own_blocks,), jnp.int32),
            pltpu.VMEM(w_qkv.shape, w_qkv.dtype),
            pltpu.VMEM(w_out.shape, w_out.dtype),
            pltpu.VMEM((slots * BLOCK, 2 * width), jnp.bfloat16),
            pltpu.VMEM((2, CHUNK * BLOCK, width), jnp.bfloat16),
            pltpu.VMEM((own_blocks, pairs, 2 * BLOCK, 2 * HEAD_DIM), jnp.bfloat16),
            pltpu.VMEM((pairs, 2 * BLOCK, BLOCK), jnp.float32),
            pltpu.VMEM((pairs, 2 * BLOCK, 4 * HEAD_DIM), jnp.float32),
            pltpu.VMEM((rows, width), jnp.bfloat16),
            pltpu.SemaphoreType.DMA((2, CHUNK)),
            pltpu.SemaphoreType.DMA((3,)),
        ],
        compiler_params=pltpu.CompilerParams(vmem_limit_bytes=limit),
        cost_estimate=pl.CostEstimate(
            flops=20_000_000_000, bytes_accessed=20_000_000, transcendentals=10_000_000
        ),
    )(turn_id, speaker, ref_flag, own, gathered, w_qkv, w_out, frames, modulation)


def per_device(frames, modulation, w_qkv, w_out, turn_id, speaker, ref_flag):
    modded = modulate(frames, modulation)
    gathered = exchange(modded, ref_flag)
    return attend(modded, gathered, w_qkv, w_out, frames, modulation, turn_id, speaker, ref_flag)


def solution(mesh):
    return jax.shard_map(
        per_device,
        mesh=mesh,
        in_specs=(
            P(("parts", "blk", "heads"), None),
            P("parts", None),
            P(),
            P(),
            P("parts"),
            P("parts"),
            P("parts"),
        ),
        out_specs=P(("parts", "blk", "heads"), None),
        check_vma=False,
    )
```

```python
import jax
import jax.numpy as jnp
from jax import lax
from jax.experimental import pallas as pl
from jax.experimental.pallas import tpu as pltpu
from jax.sharding import PartitionSpec as P

HEAD_DIM = 64
BLOCK = 128
TURN_MAX = 12
REF_DEV = 2
CHUNK = 4
WIDE = 4

norm_eps = 1e-06
score_factor = HEAD_DIM ** (-0.5) * 1.4426950408889634


def modulate_kernel(frames, modulation, modded):
    step = BLOCK // 2

    def some_rows(r, _):
        at = pl.ds(pl.multiple_of(r * step, step), step)
        widened = frames[at].astype(jnp.float32)
        average = jnp.mean(widened, axis=1, keepdims=True)
        centered = widened - average
        variance = jnp.mean(centered * centered, axis=1, keepdims=True)
        normed = centered * lax.rsqrt(variance + norm_eps)
        modded[at] = (normed * (1.0 + modulation[1:2]) + modulation[0:1]).astype(jnp.bfloat16)
        return 0

    lax.fori_loop(0, frames.shape[0] // step, some_rows, 0)


def modulate(frames, modulation):
    vmem = pl.BlockSpec(memory_space=pltpu.VMEM)
    return pl.pallas_call(
        modulate_kernel,
        out_shape=jax.ShapeDtypeStruct(frames.shape, jnp.bfloat16),
        in_specs=[vmem, vmem],
        out_specs=vmem,
    )(frames, modulation)


def exchange_kernel(
    ref_flag, own, gathered, group, staged, near_sems, relay_sems, near_twin_sems, twin_sems,
    line_sems, mate_sems, far_twin_sems, local_sems,
):
    rows = own.shape[0]
    groups = lax.axis_size("blk")
    cores = lax.axis_size("heads")
    hops = groups // 2 - 1
    blocks = cores * rows // BLOCK
    far_first = 5 * cores * rows
    g = lax.axis_index("blk")
    c = lax.axis_index("heads")
    twin = {"heads": 1 - c}
    mate = g + 1 - 2 * lax.rem(g, 2)

    def inside(q):
        return (q >= 0) & (q < groups)

    def is_far(a, b):
        return (a - b >= 3) | (b - a >= 3)

    def near_at(offset, core):
        start = pl.multiple_of((offset + 2) * cores * rows + core * rows, BLOCK)
        return gathered.at[pl.ds(start, rows)]

    def far_at(source, core):
        start = pl.multiple_of(far_first + (source * cores + core) * BLOCK, BLOCK)
        return gathered.at[pl.ds(start, BLOCK)]

    def remote(src, dst, sems, index, device):
        return pltpu.make_async_remote_copy(
            src_ref=src, dst_ref=dst, send_sem=sems.at[(0, *index)], recv_sem=sems.at[(1, *index)],
            device_id=device, device_id_type=pl.DeviceIdType.MESH,
        )

    half_rows = rows // 2
    toward = mate - g

    def half_at(offset, core, half):
        start = (offset + 2) * cores * rows + core * rows + half * half_rows
        return gathered.at[pl.ds(pl.multiple_of(start, half_rows), half_rows)]

    def near_send(offset, half):
        return remote(
            own.at[pl.ds(half * half_rows, half_rows)], half_at(-offset, c, half),
            near_sems, (2 - offset, half), {"blk": g + offset},
        )

    def relay(half):
        if half == 0:
            src, seen, device = half_at(2 * toward, c, 0), toward, mate
        else:
            src, seen, device = half_at(toward, c, 1), -toward, g + 2 * toward
        return pltpu.make_async_remote_copy(
            src_ref=src, dst_ref=half_at(seen, c, half), send_sem=relay_sems.at[half],
            recv_sem=near_sems.at[1, 2 + seen, half], device_id={"blk": device},
            device_id_type=pl.DeviceIdType.MESH,
        )

    def near_twin(offset, half):
        ref = half_at(offset, c, half)
        return remote(ref, ref, near_twin_sems, (2 + offset, half), twin)

    def line_send(way, hop, source):
        src = staged if hop == 1 else far_at(source, c)
        return remote(src, far_at(source, c), line_sems, (way, hop), {"blk": g + 2 - 4 * way})

    def mate_send(source):
        return remote(far_at(source, c), far_at(source, c), mate_sems, (source,), {"blk": mate})

    def far_twin(source):
        return remote(far_at(source, c), far_at(source, c), far_twin_sems, (source,), twin)

    sides = (2 * toward, -2 * toward)
    others = (toward, -toward, *sides)
    barrier = pltpu.get_barrier_semaphore()
    pl.semaphore_signal(barrier, inc=1, device_id=twin, device_id_type=pl.DeviceIdType.MESH)
    pl.semaphore_signal(
        barrier, inc=1, device_id={"blk": mate}, device_id_type=pl.DeviceIdType.MESH
    )
    for offset in sides:
        @pl.when(inside(g + offset))
        def _():
            pl.semaphore_signal(
                barrier, inc=1, device_id={"blk": g + offset}, device_id_type=pl.DeviceIdType.MESH
            )
    peers = 2 + sum(jnp.where(inside(g + offset), 1, 0).astype(jnp.int32) for offset in sides)
    pl.semaphore_wait(barrier, peers)

    to_twin = remote(own, group.at[c], twin_sems, (), twin)
    to_twin.start()
    near_send(toward, 1).start()
    for half in range(2):
        for offset in reversed(sides):
            @pl.when(inside(g + offset))
            def _():
                near_send(offset, half).start()
        if half == 0:
            near_send(toward, 0).start()
    keep = pltpu.make_async_copy(own, near_at(0, c), local_sems.at[0])
    keep.start()
    mine = pltpu.make_async_copy(own, group.at[c], local_sems.at[1])
    mine.start()
    mine.wait()
    to_twin.wait_recv()
    keep_twin = pltpu.make_async_copy(group.at[1 - c], near_at(0, 1 - c), local_sems.at[2])
    keep_twin.start()

    rank = jnp.int32(0)
    chosen = group[0, :BLOCK]
    for b in range(blocks):
        flag = ref_flag[g * blocks + b]
        first = (b * BLOCK) % rows
        tile = group[(b * BLOCK) // rows, first : first + BLOCK]
        chosen = jnp.where((flag == 1) & (rank == c), tile, chosen)
        rank = rank + flag
    staged[...] = chosen

    def each_line(act):
        for hop in range(1, hops + 1):
            for way in range(2):
                act(hop, way, g - 2 * hop if way == 0 else g + 2 * hop)

    for way in range(2):
        @pl.when(inside(g + 2 - 4 * way))
        def _():
            line_send(way, 1, g).start()

    def pass_on(hop, way, source):
        @pl.when(inside(source))
        def _():
            line_send(way, hop, source).wait_recv()
            if hop < hops:
                @pl.when(inside(g + 2 - 4 * way))
                def _():
                    line_send(way, hop + 1, source).start()

            @pl.when(is_far(source, mate))
            def _():
                mate_send(source).start()

            if hop >= 2:
                far_twin(source).start()

    def arrive(offset, half):
        near_send(-offset, half).wait_recv()
        near_twin(offset, half).start()

    arrive(toward, 1)

    @pl.when(inside(g + 2 * toward))
    def _():
        relay(1).start()
        arrive(2 * toward, 0)
        relay(0).start()

    each_line(pass_on)
    arrive(toward, 0)

    @pl.when(inside(g + 2 * toward))
    def _():
        arrive(2 * toward, 1)

    @pl.when(inside(g - 2 * toward))
    def _():
        arrive(-2 * toward, 0)
        arrive(-2 * toward, 1)

    def each_mate(act):
        for k in range(-hops, hops + 1):
            source = mate + 2 * k

            @pl.when(inside(source) & is_far(source, g))
            def _():
                act(source)

    def from_mate(source):
        mate_send(source).wait_recv()
        far_twin(source).start()

    each_mate(from_mate)

    @pl.when(inside(g - toward))
    def _():
        arrive(-toward, 0)
        arrive(-toward, 1)

    def finish_line(hop, way, source):
        @pl.when(inside(source))
        def _():
            if hop < hops:
                @pl.when(inside(g + 2 - 4 * way))
                def _():
                    line_send(way, hop + 1, source).wait_send()

            @pl.when(is_far(source, mate))
            def _():
                mate_send(source).wait_send()

            if hop >= 2:
                far_twin(source).wait()

    for way in range(2):
        @pl.when(inside(g + 2 - 4 * way))
        def _():
            line_send(way, 1, g).wait_send()
    each_line(finish_line)
    each_mate(lambda source: far_twin(source).wait())
    for offset in others:
        @pl.when(inside(g + offset))
        def _():
            for half in range(2):
                near_twin(offset, half).wait()

    for half in range(2):
        near_send(toward, half).wait_send()
        for offset in sides:
            @pl.when(inside(g + offset))
            def _():
                near_send(offset, half).wait_send()

        @pl.when(inside(g + 2 * toward))
        def _():
            relay(half).wait_send()
    to_twin.wait_send()
    keep.wait()
    keep_twin.wait()


def exchange(modded, ref_flag):
    rows, width = modded.shape
    groups = lax.axis_size("blk")
    cores = lax.axis_size("heads")
    dma = pltpu.SemaphoreType.DMA
    return pl.pallas_call(
        exchange_kernel,
        out_shape=jax.ShapeDtypeStruct(
            (5 * cores * rows + groups * REF_DEV * BLOCK, width), modded.dtype
        ),
        in_specs=[
            pl.BlockSpec(memory_space=pltpu.SMEM),
            pl.BlockSpec(memory_space=pltpu.VMEM),
        ],
        out_specs=pl.BlockSpec(memory_space=pl.ANY),
        scratch_shapes=[
            pltpu.VMEM((cores, rows, width), modded.dtype),
            pltpu.VMEM((BLOCK, width), modded.dtype),
            dma((2, 5, 2)),
            dma((2,)),
            dma((2, 5, 2)),
            dma((2,)),
            dma((2, 2, groups // 2)),
            dma((2, groups)),
            dma((2, groups)),
            dma((3,)),
        ],
        compiler_params=pltpu.CompilerParams(
            collective_id=0, has_side_effects=True, vmem_limit_bytes=58 * 1024 * 1024
        ),
    )(ref_flag, modded)


def attend_kernel(
    turn, speaker, ref_flag, own, gathered, w_qkv_far, w_out_far, frames, modulation, out,
    need, lists, counts, w_qkv, w_out, kv, held, queries, top, weighted, attended,
    sems, weight_sems,
):
    blocks = turn.shape[0]
    width = own.shape[1]
    own_blocks = own.shape[0] // BLOCK
    pairs = width // (2 * HEAD_DIM)
    list_len = lists.shape[0] // own_blocks
    cores = lax.axis_size("heads")
    group_blocks = cores * own_blocks
    group = lax.axis_index("blk")
    device = group * cores + lax.axis_index("heads")
    first = device * own_blocks

    weights_in = [
        pltpu.make_async_copy(
            w_qkv_far.at[:, pl.ds(0, width)], w_qkv.at[:, pl.ds(0, width)], weight_sems.at[0]
        ),
        pltpu.make_async_copy(
            w_qkv_far.at[:, pl.ds(width, 2 * width)],
            w_qkv.at[:, pl.ds(width, 2 * width)],
            weight_sems.at[1],
        ),
        pltpu.make_async_copy(w_out_far, w_out, weight_sems.at[2]),
    ]
    for copy in weights_in:
        copy.start()

    def scan_block(b, filled):
        slot, rank, lengths = filled[0], filled[1], filled[2:]
        source = b // group_blocks
        inner = b - source * group_blocks
        rank = jnp.where(inner == 0, 0, rank)
        offset = source - group
        near = (offset >= -2) & (offset <= 2)
        place = jnp.where(
            near, (offset + 2) * group_blocks + inner, 5 * group_blocks + source * REF_DEV + rank
        )
        used = jnp.int32(0)
        updated = []
        for i in range(own_blocks):
            fits = (turn[b] == turn[first + i]) | (
                (ref_flag[b] == 1) & (speaker[b] == speaker[first + i])
            )
            hit = jnp.where(fits, 1, 0).astype(jnp.int32)
            lists[i * list_len + lengths[i]] = slot
            updated.append(lengths[i] + hit)
            used = used | hit
        need[slot] = place
        return (slot + used, rank + ref_flag[b], *updated)

    zero = jnp.int32(0)
    filled = lax.fori_loop(0, blocks, scan_block, (zero,) * (own_blocks + 2), unroll=True)
    needed = filled[0]
    for i in range(own_blocks):
        length = filled[2 + i]
        counts[i] = length
        lists[i * list_len + length] = lists[i * list_len + length - 1]
    for extra in range(CHUNK):
        need[needed + extra] = need[needed - 1]
    chunks = (needed + CHUNK - 1) // CHUNK

    def fetch(chunk, side):
        return [
            pltpu.make_async_copy(
                gathered.at[pl.ds(pl.multiple_of(need[chunk * CHUNK + k] * BLOCK, BLOCK), BLOCK)],
                held.at[side, pl.ds(k * BLOCK, BLOCK)],
                sems.at[side, k],
            )
            for k in range(CHUNK)
        ]

    for copy in fetch(0, 0):
        copy.start()

    lane = lax.broadcasted_iota(jnp.int32, (BLOCK, 2 * HEAD_DIM), 1)
    lower = lane < HEAD_DIM
    step = 512

    weights_in[0].wait()
    for col in range(0, width, step):
        part = jnp.dot(
            own[...], w_qkv[:, col : col + step], preferred_element_type=jnp.float32
        ).astype(jnp.bfloat16)
        for i in range(own_blocks):
            for local in range(step // (2 * HEAD_DIM)):
                tile = part[i * BLOCK : (i + 1) * BLOCK, local * 128 : (local + 1) * 128]
                p = col // (2 * HEAD_DIM) + local
                queries[i, p, :BLOCK] = jnp.where(lower, tile, 0).astype(jnp.bfloat16)
                queries[i, p, BLOCK:] = jnp.where(lower, 0, tile).astype(jnp.bfloat16)

    weights_in[1].wait()

    def project(chunk, _):
        side = lax.rem(chunk, 2)

        @pl.when(chunk + 1 < chunks)
        def _():
            for copy in fetch(chunk + 1, 1 - side):
                copy.start()

        for copy in fetch(chunk, side):
            copy.wait()
        rows = held[side]
        for col in range(0, 2 * width, step):
            part = jnp.dot(
                rows, w_qkv[:, width + col : width + col + step],
                preferred_element_type=jnp.float32,
            ).astype(jnp.bfloat16)
            kv[pl.ds(pl.multiple_of(chunk * CHUNK * BLOCK, BLOCK), CHUNK * BLOCK), col : col + step] = part
        return 0

    lax.fori_loop(0, chunks, project, 0)

    ones = jnp.ones((WIDE * BLOCK, 128), jnp.bfloat16)

    def one_query_block(i, _):
        length = counts[i]

        def rows_of(t):
            start = lists[i * list_len + t]
            return pl.ds(pl.multiple_of(start * BLOCK, BLOCK), BLOCK)

        def side_by_side(rows, col):
            return jnp.concatenate([kv[r, col : col + 128] for r in rows], axis=0)

        def score(p, rows):
            return lax.dot_general(
                queries[i, p], side_by_side(rows, p * 128), (((1,), (1,)), ((), ())),
                preferred_element_type=jnp.float32,
            )

        def add_up(rows):
            for p in range(pairs):
                s = score(p, rows)
                weights = [
                    jnp.exp2((s[:, k * BLOCK : (k + 1) * BLOCK] - top[p]) * score_factor)
                    for k in range(len(rows))
                ]
                rounded = jnp.concatenate([w.astype(jnp.bfloat16) for w in weights], axis=1)
                values = jnp.concatenate(
                    [side_by_side(rows, width + p * 128), ones[: len(rows) * BLOCK]], axis=1
                )
                weighted[p] += jnp.dot(rounded, values, preferred_element_type=jnp.float32)

        def find_top(t, _):
            rows = [rows_of(jnp.minimum(WIDE * t + k, length - 1)) for k in range(WIDE)]
            for p in range(pairs):
                s = score(p, rows)
                high = top[p]
                for k in range(WIDE):
                    high = jnp.maximum(high, s[:, k * BLOCK : (k + 1) * BLOCK])
                top[p] = high
            return 0

        def several(t, _):
            add_up([rows_of(WIDE * t + k) for k in range(WIDE)])
            return 0

        weighted[...] = jnp.zeros(weighted.shape, jnp.float32)
        top[...] = jnp.full(top.shape, -jnp.inf, jnp.float32)
        lax.fori_loop(0, (length + WIDE - 1) // WIDE, find_top, 0)
        for p in range(pairs):
            top[p] = jnp.broadcast_to(jnp.max(top[p], axis=1, keepdims=True), top.shape[1:])
        whole = length // WIDE
        lax.fori_loop(0, whole, several, 0)
        left = length - whole * WIDE

        for rest in range(1, WIDE):
            @pl.when(left == rest)
            def _():
                add_up([rows_of(whole * WIDE + k) for k in range(rest)])

        at = pl.ds(pl.multiple_of(i * BLOCK, BLOCK), BLOCK)
        for p in range(pairs):
            ratio = weighted[p, :, :128] / weighted[p, :, 128:]
            attended[at, p * 128 : (p + 1) * 128] = jnp.where(
                lower, ratio[:BLOCK], ratio[BLOCK:]
            ).astype(jnp.bfloat16)
        return 0

    lax.fori_loop(0, own_blocks, one_query_block, 0)
    weights_in[2].wait()

    for col in range(0, width, step):
        product = jnp.dot(
            attended[...], w_out[:, col : col + step], preferred_element_type=jnp.float32
        )
        out[:, col : col + step] = (
            frames[:, col : col + step].astype(jnp.float32)
            + modulation[2:3, col : col + step] * product
        ).astype(jnp.bfloat16)


def attend(own, gathered, w_qkv, w_out, frames, modulation, turn_id, speaker, ref_flag):
    rows, width = frames.shape
    blocks = turn_id.shape[0]
    own_blocks = rows // BLOCK
    groups = lax.axis_size("blk")
    most = min(blocks, own_blocks + 2 * (TURN_MAX - 1) + REF_DEV * groups)
    slots = -(-most // CHUNK) * CHUNK
    list_len = min(blocks, TURN_MAX + REF_DEV * groups) + 4
    pairs = width // (2 * HEAD_DIM)
    limit = 2 * (w_qkv.size + w_out.size + slots * BLOCK * 2 * width) + 15 * 1024 * 1024
    smem = pl.BlockSpec(memory_space=pltpu.SMEM)
    vmem = pl.BlockSpec(memory_space=pltpu.VMEM)
    return pl.pallas_call(
        attend_kernel,
        out_shape=jax.ShapeDtypeStruct(frames.shape, jnp.bfloat16),
        in_specs=[smem] * 3 + [vmem] + [pl.BlockSpec(memory_space=pl.ANY)] * 3 + [vmem] * 2,
        out_specs=vmem,
        scratch_shapes=[
            pltpu.SMEM((slots + CHUNK + 4,), jnp.int32),
            pltpu.SMEM((own_blocks * list_len,), jnp.int32),
            pltpu.SMEM((own_blocks,), jnp.int32),
            pltpu.VMEM(w_qkv.shape, w_qkv.dtype),
            pltpu.VMEM(w_out.shape, w_out.dtype),
            pltpu.VMEM((slots * BLOCK, 2 * width), jnp.bfloat16),
            pltpu.VMEM((2, CHUNK * BLOCK, width), jnp.bfloat16),
            pltpu.VMEM((own_blocks, pairs, 2 * BLOCK, 2 * HEAD_DIM), jnp.bfloat16),
            pltpu.VMEM((pairs, 2 * BLOCK, BLOCK), jnp.float32),
            pltpu.VMEM((pairs, 2 * BLOCK, 4 * HEAD_DIM), jnp.float32),
            pltpu.VMEM((rows, width), jnp.bfloat16),
            pltpu.SemaphoreType.DMA((2, CHUNK)),
            pltpu.SemaphoreType.DMA((3,)),
        ],
        compiler_params=pltpu.CompilerParams(vmem_limit_bytes=limit),
        cost_estimate=pl.CostEstimate(
            flops=20_000_000_000, bytes_accessed=20_000_000, transcendentals=10_000_000
        ),
    )(turn_id, speaker, ref_flag, own, gathered, w_qkv, w_out, frames, modulation)


def per_device(frames, modulation, w_qkv, w_out, turn_id, speaker, ref_flag):
    modded = modulate(frames, modulation)
    gathered = exchange(modded, ref_flag)
    return attend(modded, gathered, w_qkv, w_out, frames, modulation, turn_id, speaker, ref_flag)


def solution(mesh):
    return jax.shard_map(
        per_device,
        mesh=mesh,
        in_specs=(
            P(("parts", "blk", "heads"), None),
            P("parts", None),
            P(),
            P(),
            P("parts"),
            P("parts"),
            P("parts"),
        ),
        out_specs=P(("parts", "blk", "heads"), None),
        check_vma=False,
    )
```
